512 devices in a mesh: band: 128 (over y, z, core), lon: 4 (over x).
Axes of the slice: x: 4, y: 8, z: 8, core: 2. Of those that a mesh axis runs over, the one named last changes fastest.
Arguments:
- qu_values: float32 [2, 131072, 128], P(None, ('band', 'lon')), may hold values from -1.5 to 1.5
- tap_offsets: float32 [2, 131072, 128], P(None, ('band', 'lon')), may hold values from 0 to 1
- row_base: int32 [131072, 128], P(('band', 'lon')), may hold values from 0 to 8
- col_base: int32 [131072, 128], P(('band', 'lon')), may hold values from 0 to 120
- tile_of_block: int32 [131072], P(('band', 'lon')), may hold values from 0 to 63, as said below
- m_orders: int32 [1024], replicated, may hold values from 0 to 4095, as said below
Outputs:
- spectra: float32 [1024, 4, 4096], P(('band', 'lon'))
The draws below stay inside these ranges and needn't reach their ends.
Inputs may be any that keep to these rules, and one draw needn't show every extreme that they name: `tile_of_block`: tiles of a band and longitude block are numbered row-major over (4) tile rows of 8192 // (4 * 128) tiles; the first and last tile rows lie in the neighbouring bands. Blocks of the first band never name the first tile row, blocks of the last band never the last. `m_orders`: entries 2k and 2k + 1 sum to 4095; all entries are distinct when 1024 <= 4096.
All inputs are finite; a program needn't handle non-finite values.
Results may differ from the reference program's by a relative error of at most 0.0001.
Values sent between devices are 32-bit elements; how exact they have to be, the bound alone decides.
A program may use at most 64 MiB of HBM per device.

```python
import math
import jax
import jax.numpy as jnp
from jax import lax

LL = 4096
NPHI = 8192
ROWS_DEV = 32
TR = 16
TC = 128
SLOTS = 128
NBLK = 256
NTH = 4096
MTOT = 1024
PIXROWS = 131072
N_BAND = 128
N_LON = 4


def draw_tile_of_block(key, part):
    key = jax.random.fold_in(key, 11)
    tile_cols = NPHI // (N_LON * TC)
    tile_rows = ROWS_DEV // TR + 2
    tile_count = tile_rows * tile_cols
    block_total = NBLK * N_BAND * N_LON
    tiles = jax.random.randint(key, (block_total,), 0, tile_count, dtype=jnp.int32)
    band_index = jnp.arange(block_total, dtype=jnp.int32) // (NBLK * N_LON)
    tile_row = tiles // tile_cols
    tiles = jnp.where((band_index == 0) & (tile_row == 0), tiles + tile_cols, tiles)
    tiles = jnp.where((band_index == N_BAND - 1) & (tile_row == tile_rows - 1), tiles - tile_cols, tiles)
    tiles = tiles.at[0].set(tile_count - 1)
    tiles = tiles.at[NBLK * N_LON].set(0)
    return tiles.astype(jnp.int32)


def draw_m_orders(key, part):
    key = jax.random.fold_in(key, 23)
    first_key, second_key = jax.random.split(key)
    half_count = LL // 2
    pair_count = MTOT // 2
    ordering = jax.random.permutation(first_key, half_count).astype(jnp.int32)
    zero_place = jnp.argmax(ordering == 0)
    ordering = ordering.at[zero_place].set(ordering[0]).at[0].set(0)
    picked = ordering[jnp.arange(pair_count) % half_count]
    picked = jax.random.permutation(second_key, picked)
    return jnp.stack([picked, LL - 1 - picked], axis=1).reshape(MTOT).astype(jnp.int32)


def set_ends(array, key, low, top_value):
    dims = array.shape
    index_at = [jax.random.randint(jax.random.fold_in(key, axis), (), 0, dims[axis]) for axis in range(len(dims))]
    array = array.at[tuple(index_at)].set(low)
    longest = dims.index(max(dims))
    index_at[longest] = (index_at[longest] + 1) % dims[longest]
    return array.at[tuple(index_at)].set(top_value)


def level_of(rng, shape, cuts, smallest, top_value):
    def one(dim, shards_of):
        draws = jax.random.uniform(jax.random.fold_in(jax.random.fold_in(rng, 6), dim), (shards_of,), jnp.float32, smallest / len(cuts), top_value / len(cuts))
        return jnp.repeat(jnp.exp(draws), shape[dim] // shards_of).reshape((-1,) + (1,) * (len(shape) - dim - 1))

    gain = one(*cuts[0])
    for cut in cuts[1:]:
        gain = gain * one(*cut)
    return gain


def centred(stream_key, dims, deviation, bound, shards=(), kind=jnp.bfloat16):
    values = deviation * jax.random.normal(stream_key, dims, jnp.float32)
    if shards:
        values = values * level_of(stream_key, dims, shards, -0.22, 0.18)
    return jnp.clip(values, -bound, bound).astype(kind)


def setup_inputs(seed: int = 0) -> dict:
    arg_keys = jax.random.split(jax.random.key(seed), 7)
    return {
        "qu_values": centred(arg_keys[0], (2, PIXROWS, SLOTS), 0.25, 1.5, ((1, 512),), jnp.float32),
        "tap_offsets": jnp.clip(1.0 * jax.random.uniform(arg_keys[1], (2, PIXROWS, SLOTS), jnp.float32) ** level_of(arg_keys[1], (2, PIXROWS, SLOTS), ((1, 512),), -0.2, 0.2), 0.0, 1.0),
        "row_base": set_ends(jax.random.randint(arg_keys[2], (PIXROWS, SLOTS), 0, TR - 7), jax.random.fold_in(arg_keys[2], 1), 0, (TR - 7) - 1).astype(jnp.int32),
        "col_base": set_ends(jax.random.randint(arg_keys[3], (PIXROWS, SLOTS), 0, TC - 7), jax.random.fold_in(arg_keys[3], 1), 0, (TC - 7) - 1).astype(jnp.int32),
        "tile_of_block": draw_tile_of_block(jax.random.fold_in(arg_keys[6], 71), 0),
        "m_orders": draw_m_orders(jax.random.fold_in(arg_keys[6], 71), 0),
    }


def tap_weights(base_index, fraction, extent):
    positions = jnp.arange(extent, dtype=jnp.int32)
    offsets = positions[None, None, :] - base_index[..., None]
    distance = offsets.astype(fraction.dtype) - 3.0 - fraction[..., None]
    inside = (offsets >= 0) & (offsets < 8)
    return jnp.where(inside, jnp.exp(-distance * distance / 8.0), 0.0)

def reference(qu_values, tap_offsets, row_base, col_base, tile_of_block, m_orders):
    float_type = qu_values.dtype
    columns = NPHI // N_LON
    tile_cols = columns // TC
    block_count = qu_values.shape[1]
    group_size = math.gcd(block_count, 4096)
    canvas = jnp.zeros((2, NTH + 2 * TR, NPHI), float_type)

    def deposit(step_index, canvas):
        first_block = step_index * group_size
        values = lax.dynamic_slice_in_dim(qu_values, first_block, group_size, 1)
        fractions = lax.dynamic_slice_in_dim(tap_offsets, first_block, group_size, 1)
        row_taps = tap_weights(lax.dynamic_slice_in_dim(row_base, first_block, group_size, 0), fractions[0], TR)
        col_taps = tap_weights(lax.dynamic_slice_in_dim(col_base, first_block, group_size, 0), fractions[1], TC)
        tile_sums = jnp.einsum('fgpr,gpc->fgrc', row_taps[None] * values[..., None], col_taps, precision=lax.Precision.HIGHEST)
        blocks = first_block + jnp.arange(group_size, dtype=jnp.int32)
        device = blocks // NBLK
        band_index = device // N_LON
        lon_index = device % N_LON
        tile_index = lax.dynamic_slice_in_dim(tile_of_block, first_block, group_size, 0)
        first_row = band_index * ROWS_DEV + tile_index // tile_cols * TR
        first_col = lon_index * columns + tile_index % tile_cols * TC
        row_index = first_row[:, None] + jnp.arange(TR, dtype=jnp.int32)[None, :]
        col_index = first_col[:, None] + jnp.arange(TC, dtype=jnp.int32)[None, :]
        return canvas.at[:, row_index[:, :, None], col_index[:, None, :]].add(tile_sums)
    canvas = lax.fori_loop(0, block_count // group_size, deposit, canvas)
    sky_grid = canvas[:, TR:TR + NTH]
    spectrum = jnp.fft.rfft(sky_grid, axis=2)
    colatitude = math.pi * (jnp.arange(NTH).astype(float_type) + 0.5) / NTH
    weight = math.pi * math.sqrt(2.0 / (NTH * NPHI)) * jnp.sin(colatitude)
    components = jnp.stack([jnp.real(spectrum[0]), jnp.imag(spectrum[0]), jnp.real(spectrum[1]), jnp.imag(spectrum[1])], 0).astype(float_type)
    picked = components[:, :, m_orders] * weight[None, :, None]
    return jnp.transpose(picked, (2, 0, 1))
```

```python
import functools, math
import jax, jax.numpy as jnp
from jax import lax
from jax.experimental import pallas as pl
from jax.experimental.pallas import tpu as pltpu
from jax.sharding import PartitionSpec as P

NPHI = 8192
ROWS_DEV = 32
TR, TC = 16, 128
MESH = pl.DeviceIdType.MESH


TAP_SCALE = -math.log2(math.e) / 8.0


def split(x):
    high = x.astype(jnp.bfloat16)
    return high, (x - high.astype(jnp.float32)).astype(jnp.bfloat16)


def cos_sin(quarters):
    whole = jnp.floor(quarters + 0.5)
    angle = (quarters - whole) * (math.pi / 2.0)
    square = angle * angle
    sine = angle * (1.0 + square * (-1.0 / 6 + square * (1.0 / 120 + square * (-1.0 / 5040))))
    cosine = 1.0 + square * (-0.5 + square * (1.0 / 24 + square * (-1.0 / 720 + square * (1.0 / 40320))))
    quadrant = whole.astype(jnp.int32)
    swapped = (quadrant & 1) != 0
    first = jnp.where(swapped, sine, cosine)
    second = jnp.where(swapped, cosine, sine)
    first = jnp.where(((quadrant + 1) & 2) != 0, -first, first)
    second = jnp.where((quadrant & 2) != 0, -second, second)
    return first, second


def nt_dot(a, b):
    return lax.dot_general(a, b, (((1,), (1,)), ((), ())), preferred_element_type=jnp.float32)


def spectra_kernel(bands, lons, subs, tiles_ref, orders_ref, out_ref, halo, order_col, t_hi, t_lo, turn, spin,
                   g_hi, g_lo, part, arrived, total, landed,
                   halo_send, halo_recv, x_send, x_recv, a_send, a_recv):
    band = lax.axis_index("band")
    lon = lax.axis_index("lon")
    per_lon = 2 * bands
    above = lax.rem(band + bands - 1, bands)
    below = lax.rem(band + 1, bands)

    barrier = pltpu.get_barrier_semaphore()

    def greet(step, carry):
        pl.semaphore_signal(barrier, inc=1, device_id=(lax.rem(band + step, bands), lon), device_id_type=MESH)
        return carry

    lax.fori_loop(1, bands, greet, 0)
    for step in range(1, lons):
        pl.semaphore_signal(barrier, inc=1, device_id=(band, lax.rem(lon + step, lons)), device_id_type=MESH)
    pl.semaphore_wait(barrier, bands - 1 + lons - 1)

    upward = pltpu.make_async_remote_copy(
        src_ref=tiles_ref.at[pl.ds(0, 16)], dst_ref=halo.at[1], send_sem=halo_send.at[0], recv_sem=halo_recv.at[1],
        device_id=(above, lon), device_id_type=MESH)
    downward = pltpu.make_async_remote_copy(
        src_ref=tiles_ref.at[pl.ds(48, 16)], dst_ref=halo.at[0], send_sem=halo_send.at[1], recv_sem=halo_recv.at[0],
        device_id=(below, lon), device_id_type=MESH)
    upward.start()
    downward.start()

    lane = lax.broadcasted_iota(jnp.int32, (1, 128), 1)
    half = lane // 64
    for row in range(8):
        order_col[pl.ds(row * 128, 128), :] = jnp.transpose(
            jnp.broadcast_to(orders_ref[pl.ds(row, 1), :].astype(jnp.float32), (128, 128)))
    cycle = band * ROWS_DEV + ((lane // 32) % 2) * TR + lane % 16
    _, sine = cos_sin((cycle.astype(jnp.float32) + 0.5) * (1.0 / 2048))
    weight = sine * (math.pi * math.sqrt(2.0 / (bands * ROWS_DEV * NPHI)))
    low_columns = lane.astype(jnp.float32) * (1.0 / 2048)
    spin_phase = (half * 1024 + lon * 2048).astype(jnp.float32) * (1.0 / 2048)

    def table(step, carry):
        ell = step // 2
        place = step % 2
        m = order_col[pl.ds(2 * ell + place, 128, stride=8), :]
        rows = pl.ds(pl.multiple_of(place * 128, 128), 128)
        for side in range(2):
            c, s = cos_sin(m * (low_columns + side * (128.0 / 2048)))
            c_hi, c_lo = split(c)
            s_hi, s_lo = split(-s)
            cols = pl.ds(side * 128, 128)
            t_hi[ell, 0, rows, cols] = c_hi
            t_lo[ell, 0, rows, cols] = c_lo
            t_hi[ell, 1, rows, cols] = s_hi
            t_lo[ell, 1, rows, cols] = s_lo
        c, s = cos_sin(m * (256.0 / 2048))
        turn[ell, 0, rows, :] = c
        turn[ell, 1, rows, :] = -s
        eighth = (m.astype(jnp.int32) & 7).astype(jnp.float32)
        c, s = cos_sin(eighth * spin_phase)
        spin[ell, 0, rows, :] = c * weight
        spin[ell, 1, rows, :] = -s * weight
        return carry

    lax.fori_loop(0, 2 * lons, table, 0)

    upward.wait_recv()
    downward.wait_recv()

    for v in range(4):
        for h in range(2):
            for tr in range(2):
                place = v * 128 + h * 64 + tr * 32
                for k in range(2):
                    tile = 2 * (v + 4 * h) + k
                    value = tiles_ref[16 * (tr + 1) + tile] + halo[tr, tile]
                    hi, lo = split(value)
                    g_hi[pl.ds(place, 32), pl.ds(k * 128, 128)] = hi
                    g_lo[pl.ds(place, 32), pl.ds(k * 128, 128)] = lo

    is_real = lane < 64

    def transform(ell):
        for place in range(2):
            rows = pl.ds(place * 128, 128)
            cs = []
            for q in range(2):
                hi = t_hi[ell, q, rows, :]
                lo = t_lo[ell, q, rows, :]
                cs.append(nt_dot(hi, g_hi[...]) + nt_dot(hi, g_lo[...]) + nt_dot(lo, g_hi[...]))
            c, s = cs
            wr = turn[ell, 0, rows, :]
            wi = turn[ell, 1, rows, :]
            re, im = c[:, 384:], s[:, 384:]
            for v in (2, 1, 0):
                re, im = (re * wr - im * wi + c[:, v * 128:v * 128 + 128],
                          re * wi + im * wr + s[:, v * 128:v * 128 + 128])
            pr = spin[ell, 0, rows, :]
            pi = spin[ell, 1, rows, :]
            zr = re * pr - im * pi
            zi = re * pi + im * pr
            zr = zr + pltpu.roll(zr, 64, 1)
            zi = zi + pltpu.roll(zi, 64, 1)
            part[ell, pl.ds(place, 128, stride=2), :] = jnp.where(is_real, zr, zi)

    per_sub = per_lon // subs
    quarter = band // (bands // subs)

    def sub_rows(sub):
        return pl.ds(pl.multiple_of(lax.rem(quarter + sub, subs) * per_sub, per_sub), per_sub)

    def over_lon(ell, source, sub):
        return pltpu.make_async_remote_copy(
            src_ref=part.at[ell, sub_rows(sub), :], dst_ref=arrived.at[source, sub_rows(sub), :],
            send_sem=x_send.at[ell, sub], recv_sem=x_recv.at[source, sub],
            device_id=(band, ell), device_id_type=MESH)

    def send_part(step, carry):
        ell = lax.rem(lon + step, lons)
        transform(ell)
        for sub in range(subs):
            over_lon(ell, lon, sub).start()
        return carry

    lax.fori_loop(1, lons, send_part, 0)
    transform(lon)

    for sub in range(subs):
        rows = sub_rows(sub)
        value = part[lon, rows, :]
        for step in range(1, lons):
            source = lax.rem(lon + step, lons)
            pltpu.make_async_remote_copy(
                src_ref=arrived.at[source, rows, :], dst_ref=arrived.at[source, rows, :],
                send_sem=x_send.at[source, sub], recv_sem=x_recv.at[source, sub],
                device_id=(band, source), device_id_type=MESH).wait_recv()
            value = value + arrived[source, rows, :]
        total[rows, :] = value
        first = lax.rem(quarter + sub, subs) * (bands // subs)

        def send_total(step, carry):
            target = first + step

            @pl.when(target != band)
            def _():
                pltpu.make_async_remote_copy(
                    src_ref=total.at[pl.ds(2 * target, 2), :], dst_ref=landed.at[pl.ds(2 * band, 2), :],
                    send_sem=a_send, recv_sem=a_recv, device_id=(target, lon), device_id_type=MESH).start()
            return carry

        lax.fori_loop(0, bands // subs, send_total, 0)

    own = pltpu.make_async_copy(total.at[pl.ds(2 * band, 2), :], landed.at[pl.ds(2 * band, 2), :], a_recv)
    own.start()
    pltpu.make_async_copy(landed, landed, a_recv).wait()

    lanes = lax.broadcasted_iota(jnp.int32, (bands // 4, 128), 1)
    for i in range(2):
        for f in range(2):
            for reim in range(2):
                value = jnp.zeros((bands // 4, 128), jnp.float32)
                for q in range(4):
                    x = landed[pl.ds(2 * q + i, bands // 4, stride=8), :]
                    for tr in range(2):
                        source = reim * 4 + tr * 2 + f
                        target = 2 * q + tr
                        moved = x if source == target else pltpu.roll(x, ((target - source) % 8) * 16, 1)
                        value = jnp.where(lanes // 16 == target, moved, value)
                for j in range(bands // 4):
                    out_ref[i, pl.ds(2 * f + reim, 1), pl.ds(j * 128, 128)] = value[j:j + 1, :]

    upward.wait_send()
    downward.wait_send()
    for step in range(1, lons):
        ell = lax.rem(lon + step, lons)
        for sub in range(subs):
            over_lon(ell, lon, sub).wait_send()
    others = pl.ds(0, per_lon - 2)
    pltpu.make_async_copy(total.at[others], total.at[others], a_send).wait()


def spectra(tiles, orders, bands, lons, subs=4, local=False):
    V = pl.BlockSpec(memory_space=pltpu.VMEM)
    f32, bf16 = jnp.float32, jnp.bfloat16
    return pl.pallas_call(
        functools.partial(spectra_kernel, bands, lons, subs),
        out_shape=jax.ShapeDtypeStruct((2, 4, bands * ROWS_DEV), f32),
        in_specs=[V, V],
        out_specs=V,
        scratch_shapes=[
            pltpu.VMEM((2, 16, 32, 128), f32),
            pltpu.VMEM((1024, 128), f32),
            pltpu.VMEM((lons, 2, 256, 256), bf16),
            pltpu.VMEM((lons, 2, 256, 256), bf16),
            pltpu.VMEM((lons, 2, 256, 128), f32),
            pltpu.VMEM((lons, 2, 256, 128), f32),
            pltpu.VMEM((512, 256), bf16),
            pltpu.VMEM((512, 256), bf16),
            pltpu.VMEM((lons, 256, 128), f32),
            pltpu.VMEM((lons, 256, 128), f32),
            pltpu.VMEM((256, 128), f32),
            pltpu.VMEM((256, 128), f32),
            pltpu.SemaphoreType.DMA((2,)),
            pltpu.SemaphoreType.DMA((2,)),
            pltpu.SemaphoreType.DMA((lons, subs)),
            pltpu.SemaphoreType.DMA((lons, subs)),
            pltpu.SemaphoreType.DMA,
            pltpu.SemaphoreType.DMA,
        ],
        compiler_params=pltpu.CompilerParams(collective_id=0, has_side_effects=True, vmem_limit_bytes=40 * 1024 * 1024),
    )(tiles, orders)


def deposit_kernel(unroll, tile_ref, qu_ref, off_ref, rb_ref, cb_ref, tiles_ref):
    tiles_ref[...] = jnp.zeros_like(tiles_ref)
    pos = lax.broadcasted_iota(jnp.int32, (16, 128), 0)

    def one(n):
        row = pl.ds(n, 1)
        cb = cb_ref[row, :]
        col_o = (pos - cb) & 15
        d = col_o.astype(jnp.float32) - (off_ref[1, row, :] + 3.0)
        v = jnp.exp2(d * d * TAP_SCALE)
        v_hi, v_lo = split(v)
        group = jnp.where(col_o < 8, cb + col_o - pos, -16).astype(jnp.bfloat16)
        zero = jnp.zeros((16, 128), jnp.bfloat16)
        hi, lo = [], []
        for ch in range(8):
            m = group == jnp.bfloat16(16 * ch)
            hi.append(jnp.where(m, v_hi, zero))
            lo.append(jnp.where(m, v_lo, zero))
        cols = jnp.concatenate([jnp.concatenate(hi, 0), jnp.concatenate(lo, 0)], 1)
        row_o = (pos - rb_ref[row, :]) & 15
        e = row_o.astype(jnp.float32) - (off_ref[0, row, :] + 3.0)
        a = jnp.where(row_o < 8, jnp.exp2(e * e * TAP_SCALE), 0.0)
        q_hi, q_lo = split(a * qu_ref[0, row, :])
        u_hi, u_lo = split(a * qu_ref[1, row, :])
        half = jnp.concatenate([q_hi, u_hi, q_lo, u_lo], 0)
        rows = jnp.concatenate([half, half], 1)
        out = lax.dot_general(rows, cols, (((1,), (1,)), ((), ())), preferred_element_type=jnp.float32)
        return out[:32] + out[32:]

    def step(i, carry):
        outs = [(tile_ref[i * unroll + j], one(i * unroll + j)) for j in range(unroll)]
        for t, o in outs:
            tiles_ref[t] += o
        return carry

    lax.fori_loop(0, 256 // unroll, step, 0)

def deposit(qu, off, rb, cb, tile, unroll=8):
    V = pl.BlockSpec(memory_space=pltpu.VMEM)
    return pl.pallas_call(
        functools.partial(deposit_kernel, unroll),
        out_shape=jax.ShapeDtypeStruct((64, 32, 128), jnp.float32),
        in_specs=[pl.BlockSpec(memory_space=pltpu.SMEM), V, V, V, V],
        out_specs=V,
    )(tile, qu, off, rb, cb)


def body(qu_values, tap_offsets, row_base, col_base, tile_of_block, m_orders):
    bands = lax.axis_size("band")
    lons = lax.axis_size("lon")
    tiles = deposit(qu_values, tap_offsets, row_base, col_base, tile_of_block, 32)
    return spectra(tiles, m_orders.reshape(8, 128), bands, lons)


def solution(mesh):
    placed = (
        P(None, ("band", "lon"), None),
        P(None, ("band", "lon"), None),
        P(("band", "lon"), None),
        P(("band", "lon"), None),
        P(("band", "lon")),
        P(),
    )
    return jax.shard_map(
        body, mesh=mesh, in_specs=placed, out_specs=P(("band", "lon"), None, None), check_vma=False
    )
```

```python
import functools, math
import jax, jax.numpy as jnp
from jax import lax
from jax.experimental import pallas as pl
from jax.experimental.pallas import tpu as pltpu
from jax.sharding import PartitionSpec as P

NPHI = 8192
ROWS_DEV = 32
TR, TC = 16, 128
MESH = pl.DeviceIdType.MESH


TAP_SCALE = -math.log2(math.e) / 8.0


def split(x):
    high = x.astype(jnp.bfloat16)
    return high, (x - high.astype(jnp.float32)).astype(jnp.bfloat16)


def cos_sin(quarters):
    whole = jnp.floor(quarters + 0.5)
    angle = (quarters - whole) * (math.pi / 2.0)
    square = angle * angle
    sine = angle * (1.0 + square * (-1.0 / 6 + square * (1.0 / 120 + square * (-1.0 / 5040))))
    cosine = 1.0 + square * (-0.5 + square * (1.0 / 24 + square * (-1.0 / 720 + square * (1.0 / 40320))))
    quadrant = whole.astype(jnp.int32)
    swapped = (quadrant & 1) != 0
    first = jnp.where(swapped, sine, cosine)
    second = jnp.where(swapped, cosine, sine)
    first = jnp.where(((quadrant + 1) & 2) != 0, -first, first)
    second = jnp.where((quadrant & 2) != 0, -second, second)
    return first, second


def nt_dot(a, b):
    return lax.dot_general(a, b, (((1,), (1,)), ((), ())), preferred_element_type=jnp.float32)


def spectra_kernel(bands, lons, subs, lag, tiles_ref, orders_ref, out_ref, halo, order_col, t_hi, t_lo, turn, spin,
                   g_hi, g_lo, part, arrived, total, landed,
                   halo_send, halo_recv, x_send, x_recv, a_send, a_recv):
    band = lax.axis_index("band")
    lon = lax.axis_index("lon")
    per_lon = 2 * bands
    run = bands // subs
    per_sub = 2 * run
    per_group = per_sub * lons
    quarter = band // run
    above = lax.rem(band + bands - 1, bands)
    below = lax.rem(band + 1, bands)

    barrier = pltpu.get_barrier_semaphore()

    def greet(step, carry):
        pl.semaphore_signal(barrier, inc=1, device_id=(lax.rem(band + step, bands), lon), device_id_type=MESH)
        return carry

    lax.fori_loop(1, bands, greet, 0)
    for step in range(1, lons):
        pl.semaphore_signal(barrier, inc=1, device_id=(band, lax.rem(lon + step, lons)), device_id_type=MESH)
    pl.semaphore_wait(barrier, bands - 1 + lons - 1)

    upward = pltpu.make_async_remote_copy(
        src_ref=tiles_ref.at[pl.ds(0, 16)], dst_ref=halo.at[1], send_sem=halo_send.at[0], recv_sem=halo_recv.at[1],
        device_id=(above, lon), device_id_type=MESH)
    downward = pltpu.make_async_remote_copy(
        src_ref=tiles_ref.at[pl.ds(48, 16)], dst_ref=halo.at[0], send_sem=halo_send.at[1], recv_sem=halo_recv.at[0],
        device_id=(below, lon), device_id_type=MESH)
    upward.start()
    downward.start()

    lane = lax.broadcasted_iota(jnp.int32, (1, 128), 1)
    half = lane // 64
    for row in range(8):
        order_col[pl.ds(row * 128, 128), :] = jnp.transpose(
            jnp.broadcast_to(orders_ref[pl.ds(row, 1), :].astype(jnp.float32), (128, 128)))
    cycle = band * ROWS_DEV + ((lane // 32) % 2) * TR + lane % 16
    _, sine = cos_sin((cycle.astype(jnp.float32) + 0.5) * (1.0 / 2048))
    weight = sine * (math.pi * math.sqrt(2.0 / (bands * ROWS_DEV * NPHI)))
    low_columns = lane.astype(jnp.float32) * (1.0 / 2048)
    spin_phase = (half * 1024 + lon * 2048).astype(jnp.float32) * (1.0 / 2048)

    def table(step, carry):
        group = step // lons
        ell = lax.rem(step, lons)
        first = group * per_group + 2 * ell
        m = jnp.concatenate([order_col[pl.ds(first + place, run, stride=2 * lons), :] for place in range(2)], 0)
        rows = pl.ds(pl.multiple_of(ell * 2 * run, 2 * run), 2 * run)
        for side in range(2):
            c, s = cos_sin(m * (low_columns + side * (128.0 / 2048)))
            c_hi, c_lo = split(c)
            s_hi, s_lo = split(-s)
            cols = pl.ds(side * 128, 128)
            t_hi[group, 0, rows, cols] = c_hi
            t_lo[group, 0, rows, cols] = c_lo
            t_hi[group, 1, rows, cols] = s_hi
            t_lo[group, 1, rows, cols] = s_lo
        c, s = cos_sin(m * (256.0 / 2048))
        turn[group, 0, rows, :] = c
        turn[group, 1, rows, :] = -s
        eighth = (m.astype(jnp.int32) & 7).astype(jnp.float32)
        c, s = cos_sin(eighth * spin_phase)
        spin[group, 0, rows, :] = c * weight
        spin[group, 1, rows, :] = -s * weight
        return carry

    lax.fori_loop(0, subs * lons, table, 0)

    upward.wait_recv()
    downward.wait_recv()

    for v in range(4):
        for h in range(2):
            for tr in range(2):
                place = v * 128 + h * 64 + tr * 32
                for k in range(2):
                    tile = 2 * (v + 4 * h) + k
                    value = tiles_ref[16 * (tr + 1) + tile] + halo[tr, tile]
                    hi, lo = split(value)
                    g_hi[pl.ds(place, 32), pl.ds(k * 128, 128)] = hi
                    g_lo[pl.ds(place, 32), pl.ds(k * 128, 128)] = lo

    is_real = lane < 64

    def transform(group):
        for side in range(2):
            rows = pl.ds(side * 128, 128)
            cs = []
            for q in range(2):
                hi = t_hi[group, q, rows, :]
                lo = t_lo[group, q, rows, :]
                cs.append(nt_dot(hi, g_hi[...]) + nt_dot(hi, g_lo[...]) + nt_dot(lo, g_hi[...]))
            c, s = cs
            wr = turn[group, 0, rows, :]
            wi = turn[group, 1, rows, :]
            re, im = c[:, 384:], s[:, 384:]
            for v in (2, 1, 0):
                re, im = (re * wr - im * wi + c[:, v * 128:v * 128 + 128],
                          re * wi + im * wr + s[:, v * 128:v * 128 + 128])
            pr = spin[group, 0, rows, :]
            pi = spin[group, 1, rows, :]
            zr = re * pr - im * pi
            zi = re * pi + im * pr
            zr = zr + pltpu.roll(zr, 64, 1)
            zi = zi + pltpu.roll(zi, 64, 1)
            z = jnp.where(is_real, zr, zi)
            for k in range(128 // run):
                ell, place = divmod(side * (128 // run) + k, 2)
                part[group, ell, pl.ds(place, run, stride=2), :] = z[k * run:(k + 1) * run]

    def over_lon(step, group, sub):
        ell = lax.rem(lon + step, lons)
        return pltpu.make_async_remote_copy(
            src_ref=part.at[group, ell], dst_ref=arrived.at[group, lons - step],
            send_sem=x_send.at[step, sub], recv_sem=x_recv.at[lons - step, sub],
            device_id=(band, ell), device_id_type=MESH)

    def send_part(sub, carry):
        group = lax.rem(quarter + sub, subs)
        transform(group)
        for step in (2, 1, 3):
            over_lon(step, group, sub).start()
        return carry

    def send_total(sub, carry):
        group = lax.rem(quarter + sub, subs)
        value = part[group, lon]
        for step in range(1, lons):
            over_lon(step, group, sub).wait_recv()
            value = value + arrived[group, lons - step]
        rows = pl.ds(pl.multiple_of(group * per_sub, per_sub), per_sub)
        total[rows, :] = value

        def send_one(step, carry):
            target = group * run + lax.rem(band + step, run)

            @pl.when(target != band)
            def _():
                pltpu.make_async_remote_copy(
                    src_ref=total.at[pl.ds(2 * target, 2), :], dst_ref=landed.at[pl.ds(2 * band, 2), :],
                    send_sem=a_send, recv_sem=a_recv, device_id=(target, lon), device_id_type=MESH).start()
            return carry

        return lax.fori_loop(0, run, send_one, carry)

    def pipeline(sub, carry):
        @pl.when(sub < subs)
        def _():
            send_part(sub, 0)

        @pl.when(sub >= lag)
        def _():
            send_total(sub - lag, 0)
        return carry

    lax.fori_loop(0, subs + lag, pipeline, 0)

    own = pltpu.make_async_copy(total.at[pl.ds(2 * band, 2), :], landed.at[pl.ds(2 * band, 2), :], a_recv)
    own.start()
    pltpu.make_async_copy(landed, landed, a_recv).wait()

    lanes = lax.broadcasted_iota(jnp.int32, (bands // 4, 128), 1)
    for i in range(2):
        for f in range(2):
            for reim in range(2):
                value = jnp.zeros((bands // 4, 128), jnp.float32)
                for q in range(4):
                    x = landed[pl.ds(2 * q + i, bands // 4, stride=8), :]
                    for tr in range(2):
                        source = reim * 4 + tr * 2 + f
                        target = 2 * q + tr
                        moved = x if source == target else pltpu.roll(x, ((target - source) % 8) * 16, 1)
                        value = jnp.where(lanes // 16 == target, moved, value)
                for j in range(bands // 4):
                    out_ref[i, pl.ds(2 * f + reim, 1), pl.ds(j * 128, 128)] = value[j:j + 1, :]

    upward.wait_send()
    downward.wait_send()
    for sub in range(subs):
        for step in range(1, lons):
            over_lon(step, lax.rem(quarter + sub, subs), sub).wait_send()
    others = pl.ds(0, per_lon - 2)
    pltpu.make_async_copy(total.at[others], total.at[others], a_send).wait()


def spectra(tiles, orders, bands, lons, subs=4, lag=2):
    V = pl.BlockSpec(memory_space=pltpu.VMEM)
    f32, bf16 = jnp.float32, jnp.bfloat16
    return pl.pallas_call(
        functools.partial(spectra_kernel, bands, lons, subs, lag),
        out_shape=jax.ShapeDtypeStruct((2, 4, bands * ROWS_DEV), f32),
        in_specs=[V, V],
        out_specs=V,
        scratch_shapes=[
            pltpu.VMEM((2, 16, 32, 128), f32),
            pltpu.VMEM((1024, 128), f32),
            pltpu.VMEM((subs, 2, 256, 256), bf16),
            pltpu.VMEM((subs, 2, 256, 256), bf16),
            pltpu.VMEM((subs, 2, 256, 128), f32),
            pltpu.VMEM((subs, 2, 256, 128), f32),
            pltpu.VMEM((512, 256), bf16),
            pltpu.VMEM((512, 256), bf16),
            pltpu.VMEM((subs, lons, 256 // subs, 128), f32),
            pltpu.VMEM((subs, lons, 256 // subs, 128), f32),
            pltpu.VMEM((256, 128), f32),
            pltpu.VMEM((256, 128), f32),
            pltpu.SemaphoreType.DMA((2,)),
            pltpu.SemaphoreType.DMA((2,)),
            pltpu.SemaphoreType.DMA((lons, subs)),
            pltpu.SemaphoreType.DMA((lons, subs)),
            pltpu.SemaphoreType.DMA,
            pltpu.SemaphoreType.DMA,
        ],
        compiler_params=pltpu.CompilerParams(collective_id=0, has_side_effects=True, vmem_limit_bytes=40 * 1024 * 1024),
    )(tiles, orders)


def deposit_kernel(unroll, tile_ref, qu_ref, off_ref, rb_ref, cb_ref, tiles_ref):
    tiles_ref[...] = jnp.zeros_like(tiles_ref)
    pos = lax.broadcasted_iota(jnp.int32, (16, 128), 0)

    def one(n):
        row = pl.ds(n, 1)
        cb = cb_ref[row, :]
        col_o = (pos - cb) & 15
        d = col_o.astype(jnp.float32) - (off_ref[1, row, :] + 3.0)
        v = jnp.exp2(d * d * TAP_SCALE)
        v_hi, v_lo = split(v)
        group = jnp.where(col_o < 8, cb + col_o - pos, -16).astype(jnp.bfloat16)
        zero = jnp.zeros((16, 128), jnp.bfloat16)
        hi, lo = [], []
        for ch in range(8):
            m = group == jnp.bfloat16(16 * ch)
            hi.append(jnp.where(m, v_hi, zero))
            lo.append(jnp.where(m, v_lo, zero))
        cols = jnp.concatenate([jnp.concatenate(hi, 0), jnp.concatenate(lo, 0)], 1)
        row_o = (pos - rb_ref[row, :]) & 15
        e = row_o.astype(jnp.float32) - (off_ref[0, row, :] + 3.0)
        a = jnp.where(row_o < 8, jnp.exp2(e * e * TAP_SCALE), 0.0)
        q_hi, q_lo = split(a * qu_ref[0, row, :])
        u_hi, u_lo = split(a * qu_ref[1, row, :])
        half = jnp.concatenate([q_hi, u_hi, q_lo, u_lo], 0)
        rows = jnp.concatenate([half, half], 1)
        out = lax.dot_general(rows, cols, (((1,), (1,)), ((), ())), preferred_element_type=jnp.float32)
        return out[:32] + out[32:]

    def step(i, carry):
        outs = [(tile_ref[i * unroll + j], one(i * unroll + j)) for j in range(unroll)]
        for t, o in outs:
            tiles_ref[t] += o
        return carry

    lax.fori_loop(0, 256 // unroll, step, 0)

def deposit(qu, off, rb, cb, tile, unroll=8):
    V = pl.BlockSpec(memory_space=pltpu.VMEM)
    return pl.pallas_call(
        functools.partial(deposit_kernel, unroll),
        out_shape=pltpu.VMEM((64, 32, 128), jnp.float32),
        in_specs=[pl.BlockSpec(memory_space=pltpu.SMEM), V, V, V, V],
        out_specs=V,
    )(tile, qu, off, rb, cb)


def body(qu_values, tap_offsets, row_base, col_base, tile_of_block, m_orders):
    bands = lax.axis_size("band")
    lons = lax.axis_size("lon")
    tiles = deposit(qu_values, tap_offsets, row_base, col_base, tile_of_block, 32)
    return spectra(tiles, m_orders.reshape(8, 128), bands, lons)


def solution(mesh):
    placed = (
        P(None, ("band", "lon"), None),
        P(None, ("band", "lon"), None),
        P(("band", "lon"), None),
        P(("band", "lon"), None),
        P(("band", "lon")),
        P(),
    )
    return jax.shard_map(
        body, mesh=mesh, in_specs=placed, out_specs=P(("band", "lon"), None, None), check_vma=False
    )
```

```python
import functools, math
import jax, jax.numpy as jnp
from jax import lax
from jax.experimental import pallas as pl
from jax.experimental.pallas import tpu as pltpu
from jax.sharding import PartitionSpec as P

NPHI = 8192
ROWS_DEV = 32
TR, TC = 16, 128
MESH = pl.DeviceIdType.MESH
TAP_SCALE = -math.log2(math.e) / 8.0


def split(x):
    high = x.astype(jnp.bfloat16)
    return high, (x - high.astype(jnp.float32)).astype(jnp.bfloat16)


def cos_sin(quarters):
    whole = jnp.floor(quarters + 0.5)
    angle = (quarters - whole) * (math.pi / 2.0)
    square = angle * angle
    sine = angle * (1.0 + square * (-1.0 / 6 + square * (1.0 / 120 + square * (-1.0 / 5040))))
    cosine = 1.0 + square * (-0.5 + square * (1.0 / 24 + square * (-1.0 / 720 + square * (1.0 / 40320))))
    quadrant = whole.astype(jnp.int32)
    swapped = (quadrant & 1) != 0
    first = jnp.where(swapped, sine, cosine)
    second = jnp.where(swapped, cosine, sine)
    first = jnp.where(((quadrant + 1) & 2) != 0, -first, first)
    second = jnp.where((quadrant & 2) != 0, -second, second)
    return first, second


def nt_dot(a, b):
    return lax.dot_general(a, b, (((1,), (1,)), ((), ())), preferred_element_type=jnp.float32)


def spectra_kernel(bands, lons, subs, lag, unroll, target_ref, qu_ref, off_ref, rb_ref, cb_ref, orders_ref, out_ref,
                   block_sums, tiles, halo, order_col, t_hi, t_lo, turn, spin, g_hi, g_lo, part, arrived, total, landed,
                   halo_send, halo_recv, x_send, x_recv, a_send, a_recv):
    band = lax.axis_index("band")
    lon = lax.axis_index("lon")
    run = bands // subs
    per_sub = 2 * run
    per_group = per_sub * lons
    per_lon = 2 * bands
    quarter = band // run
    above = lax.rem(band + bands - 1, bands)
    below = lax.rem(band + 1, bands)
    blocks = rb_ref.shape[0]

    barrier = pltpu.get_barrier_semaphore()
    for step in range(1, lons):
        pl.semaphore_signal(barrier, inc=1, device_id=(band, lax.rem(lon + step, lons)), device_id_type=MESH)

    pos = lax.broadcasted_iota(jnp.int32, (TR, 128), 0)

    def block_tile(n):
        row = pl.ds(n, 1)
        cb = cb_ref[row, :]
        col_o = (pos - cb) & 15
        d = col_o.astype(jnp.float32) - (off_ref[1, row, :] + 3.0)
        v_hi, v_lo = split(jnp.exp2(d * d * TAP_SCALE))
        group = jnp.where(col_o < 8, cb + col_o - pos, -16).astype(jnp.bfloat16)
        zero = jnp.zeros((TR, 128), jnp.bfloat16)
        hi, lo = [], []
        for sixteen in range(TC // 16):
            here = group == jnp.bfloat16(16 * sixteen)
            hi.append(jnp.where(here, v_hi, zero))
            lo.append(jnp.where(here, v_lo, zero))
        cols = jnp.concatenate([jnp.concatenate(hi, 0), jnp.concatenate(lo, 0)], 1)
        row_o = (pos - rb_ref[row, :]) & 15
        e = row_o.astype(jnp.float32) - (off_ref[0, row, :] + 3.0)
        a = jnp.where(row_o < 8, jnp.exp2(e * e * TAP_SCALE), 0.0)
        q_hi, q_lo = split(a * qu_ref[0, row, :])
        u_hi, u_lo = split(a * qu_ref[1, row, :])
        half = jnp.concatenate([q_hi, u_hi, q_lo, u_lo], 0)
        out = nt_dot(jnp.concatenate([half, half], 1), cols)
        return out[:2 * TR] + out[2 * TR:]

    greets = bands * unroll // blocks

    def deposit(i, carry):
        for j in range(greets):
            step = i * greets + j

            @pl.when(step > 0)
            def _():
                pl.semaphore_signal(barrier, inc=1, device_id=(lax.rem(band + step, bands), lon), device_id_type=MESH)

        for j in range(unroll):
            n = i * unroll + j
            block_sums[pl.ds(n, 2 * TR, stride=blocks), :] = block_tile(n)
        return carry

    lax.fori_loop(0, blocks // unroll, deposit, 0)

    select = jnp.where(lax.broadcasted_iota(jnp.int32, (64, blocks), 0) == target_ref[...], 1.0, 0.0).astype(jnp.bfloat16)

    def gather(pair, carry):
        pieces = [split(block_sums[pl.ds(pl.multiple_of((2 * pair + k) * blocks, blocks), blocks), :]) for k in range(2)]
        hi = jnp.concatenate([pieces[0][0], pieces[1][0]], 1)
        lo = jnp.concatenate([pieces[0][1], pieces[1][1]], 1)
        value = (jnp.dot(select, hi, preferred_element_type=jnp.float32)
                 + jnp.dot(select, lo, preferred_element_type=jnp.float32))
        for k in range(2):
            for tr in range(4):
                tiles[tr, pl.ds(pl.multiple_of((2 * pair + k) * 16, 16), 16), :] = value[tr * 16:tr * 16 + 16, k * 128:k * 128 + 128]
        return carry

    lax.fori_loop(0, TR, gather, 0)
    pl.semaphore_wait(barrier, bands - 1 + lons - 1)

    upward = pltpu.make_async_remote_copy(
        src_ref=tiles.at[0], dst_ref=halo.at[1], send_sem=halo_send.at[0], recv_sem=halo_recv.at[1],
        device_id=(above, lon), device_id_type=MESH)
    downward = pltpu.make_async_remote_copy(
        src_ref=tiles.at[3], dst_ref=halo.at[0], send_sem=halo_send.at[1], recv_sem=halo_recv.at[0],
        device_id=(below, lon), device_id_type=MESH)
    upward.start()
    downward.start()

    lane = lax.broadcasted_iota(jnp.int32, (1, 128), 1)
    half = lane // 64
    for row in range(8):
        order_col[pl.ds(row * 128, 128), :] = jnp.transpose(
            jnp.broadcast_to(orders_ref[pl.ds(row, 1), :].astype(jnp.float32), (128, 128)))
    cycle = band * ROWS_DEV + ((lane // 32) % 2) * TR + lane % 16
    _, sine = cos_sin((cycle.astype(jnp.float32) + 0.5) * (1.0 / 2048))
    weight = sine * (math.pi * math.sqrt(2.0 / (bands * ROWS_DEV * NPHI)))
    low_columns = lane.astype(jnp.float32) * (1.0 / 2048)
    spin_phase = (half * 1024 + lon * 2048).astype(jnp.float32) * (1.0 / 2048)

    def table(step, carry):
        group = step // lons
        ell = lax.rem(step, lons)
        first = group * per_group + 2 * ell
        m = jnp.concatenate([order_col[pl.ds(first + place, run, stride=2 * lons), :] for place in range(2)], 0)
        rows = pl.ds(pl.multiple_of(ell * 2 * run, 2 * run), 2 * run)
        for side in range(2):
            c, s = cos_sin(m * (low_columns + side * (128.0 / 2048)))
            c_hi, c_lo = split(c)
            s_hi, s_lo = split(-s)
            cols = pl.ds(side * 128, 128)
            t_hi[group, 0, rows, cols] = c_hi
            t_lo[group, 0, rows, cols] = c_lo
            t_hi[group, 1, rows, cols] = s_hi
            t_lo[group, 1, rows, cols] = s_lo
        c, s = cos_sin(m * (256.0 / 2048))
        turn[group, 0, rows, :] = c
        turn[group, 1, rows, :] = -s
        eighth = (m.astype(jnp.int32) & 7).astype(jnp.float32)
        c, s = cos_sin(eighth * spin_phase)
        spin[group, 0, rows, :] = c * weight
        spin[group, 1, rows, :] = -s * weight
        return carry

    lax.fori_loop(0, subs * lons, table, 0)

    upward.wait_recv()
    downward.wait_recv()

    for v in range(4):
        for h in range(2):
            for tr in range(2):
                place = v * 128 + h * 64 + tr * 32
                for k in range(2):
                    rows = pl.ds(2 * (v + 4 * h) + k, 32, stride=16)
                    value = tiles[tr + 1, rows, :] + halo[tr, rows, :]
                    hi, lo = split(value)
                    g_hi[pl.ds(place, 32), pl.ds(k * 128, 128)] = hi
                    g_lo[pl.ds(place, 32), pl.ds(k * 128, 128)] = lo

    is_real = lane < 64

    def transform(group):
        for side in range(2):
            rows = pl.ds(side * 128, 128)
            cs = []
            for q in range(2):
                hi = t_hi[group, q, rows, :]
                lo = t_lo[group, q, rows, :]
                cs.append(nt_dot(hi, g_hi[...]) + nt_dot(hi, g_lo[...]) + nt_dot(lo, g_hi[...]))
            c, s = cs
            wr = turn[group, 0, rows, :]
            wi = turn[group, 1, rows, :]
            re, im = c[:, 384:], s[:, 384:]
            for v in (2, 1, 0):
                re, im = (re * wr - im * wi + c[:, v * 128:v * 128 + 128],
                          re * wi + im * wr + s[:, v * 128:v * 128 + 128])
            pr = spin[group, 0, rows, :]
            pi = spin[group, 1, rows, :]
            zr = re * pr - im * pi
            zi = re * pi + im * pr
            zr = zr + pltpu.roll(zr, 64, 1)
            zi = zi + pltpu.roll(zi, 64, 1)
            z = jnp.where(is_real, zr, zi)
            for k in range(128 // run):
                ell, place = divmod(side * (128 // run) + k, 2)
                part[group, ell, pl.ds(place, run, stride=2), :] = z[k * run:(k + 1) * run]

    def over_lon(step, group, sub):
        ell = lax.rem(lon + step, lons)
        return pltpu.make_async_remote_copy(
            src_ref=part.at[group, ell], dst_ref=arrived.at[group, lons - step],
            send_sem=x_send.at[step, sub], recv_sem=x_recv.at[lons - step, sub],
            device_id=(band, ell), device_id_type=MESH)

    def send_part(sub, carry):
        group = lax.rem(quarter + sub, subs)
        transform(group)
        for step in (2, 1, 3):
            over_lon(step, group, sub).start()
        return carry

    def send_total(sub, carry):
        group = lax.rem(quarter + sub, subs)
        value = part[group, lon]
        for step in range(1, lons):
            over_lon(step, group, sub).wait_recv()
            value = value + arrived[group, lons - step]
        rows = pl.ds(pl.multiple_of(group * per_sub, per_sub), per_sub)
        total[rows, :] = value

        def send_one(step, carry):
            target = group * run + lax.rem(band + step, run)

            @pl.when(target != band)
            def _():
                pltpu.make_async_remote_copy(
                    src_ref=total.at[pl.ds(2 * target, 2), :], dst_ref=landed.at[pl.ds(2 * band, 2), :],
                    send_sem=a_send, recv_sem=a_recv, device_id=(target, lon), device_id_type=MESH).start()
            return carry

        return lax.fori_loop(0, run, send_one, carry)

    def pipeline(sub, carry):
        @pl.when(sub < subs)
        def _():
            send_part(sub, 0)

        @pl.when(sub >= lag)
        def _():
            send_total(sub - lag, 0)
        return carry

    lax.fori_loop(0, subs + lag, pipeline, 0)

    own = pltpu.make_async_copy(total.at[pl.ds(2 * band, 2), :], landed.at[pl.ds(2 * band, 2), :], a_recv)
    own.start()
    pltpu.make_async_copy(landed, landed, a_recv).wait()

    lanes = lax.broadcasted_iota(jnp.int32, (bands // 4, 128), 1)
    for i in range(2):
        for f in range(2):
            for reim in range(2):
                value = jnp.zeros((bands // 4, 128), jnp.float32)
                for q in range(4):
                    x = landed[pl.ds(2 * q + i, bands // 4, stride=8), :]
                    for tr in range(2):
                        source = reim * 4 + tr * 2 + f
                        target = 2 * q + tr
                        moved = x if source == target else pltpu.roll(x, ((target - source) % 8) * 16, 1)
                        value = jnp.where(lanes // 16 == target, moved, value)
                for j in range(bands // 4):
                    out_ref[i, pl.ds(2 * f + reim, 1), pl.ds(j * 128, 128)] = value[j:j + 1, :]

    upward.wait_send()
    downward.wait_send()
    for sub in range(subs):
        for step in range(1, lons):
            over_lon(step, lax.rem(quarter + sub, subs), sub).wait_send()
    others = pl.ds(0, per_lon - 2)
    pltpu.make_async_copy(total.at[others], total.at[others], a_send).wait()


def spectra(targets, qu, off, rb, cb, orders, bands, lons, subs=4, lag=2, unroll=16):
    V = pl.BlockSpec(memory_space=pltpu.VMEM)
    f32, bf16 = jnp.float32, jnp.bfloat16
    blocks = rb.shape[0]
    return pl.pallas_call(
        functools.partial(spectra_kernel, bands, lons, subs, lag, unroll),
        out_shape=jax.ShapeDtypeStruct((2, 4, bands * ROWS_DEV), f32),
        in_specs=[V] * 6,
        out_specs=V,
        scratch_shapes=[
            pltpu.VMEM((2 * TR * blocks, TC), f32),
            pltpu.VMEM((4, 512, TC), f32),
            pltpu.VMEM((2, 512, TC), f32),
            pltpu.VMEM((1024, 128), f32),
            pltpu.VMEM((subs, 2, 256, 256), bf16),
            pltpu.VMEM((subs, 2, 256, 256), bf16),
            pltpu.VMEM((subs, 2, 256, 128), f32),
            pltpu.VMEM((subs, 2, 256, 128), f32),
            pltpu.VMEM((512, 256), bf16),
            pltpu.VMEM((512, 256), bf16),
            pltpu.VMEM((subs, lons, 256 // subs, 128), f32),
            pltpu.VMEM((subs, lons, 256 // subs, 128), f32),
            pltpu.VMEM((256, 128), f32),
            pltpu.VMEM((256, 128), f32),
            pltpu.SemaphoreType.DMA((2,)),
            pltpu.SemaphoreType.DMA((2,)),
            pltpu.SemaphoreType.DMA((lons, subs)),
            pltpu.SemaphoreType.DMA((lons, subs)),
            pltpu.SemaphoreType.DMA,
            pltpu.SemaphoreType.DMA,
        ],
        compiler_params=pltpu.CompilerParams(collective_id=0, has_side_effects=True, vmem_limit_bytes=40 * 1024 * 1024),
    )(targets, qu, off, rb, cb, orders)


def body(qu_values, tap_offsets, row_base, col_base, tile_of_block, m_orders):
    bands = lax.axis_size("band")
    lons = lax.axis_size("lon")
    return spectra(tile_of_block.reshape(1, -1), qu_values, tap_offsets, row_base, col_base, m_orders.reshape(8, 128),
                   bands, lons)


def solution(mesh):
    placed = (
        P(None, ("band", "lon"), None),
        P(None, ("band", "lon"), None),
        P(("band", "lon"), None),
        P(("band", "lon"), None),
        P(("band", "lon")),
        P(),
    )
    return jax.shard_map(
        body, mesh=mesh, in_specs=placed, out_specs=P(("band", "lon"), None, None), check_vma=False
    )
```

```python
import functools, math
import jax, jax.numpy as jnp
from jax import lax
from jax.experimental import pallas as pl
from jax.experimental.pallas import tpu as pltpu
from jax.sharding import PartitionSpec as P

NPHI = 8192
ROWS_DEV = 32
TR, TC = 16, 128
MESH = pl.DeviceIdType.MESH
TAP_SCALE = -math.log2(math.e) / 8.0


def split(x):
    high = x.astype(jnp.bfloat16)
    return high, (x - high.astype(jnp.float32)).astype(jnp.bfloat16)


def cos_sin(quarters):
    whole = jnp.floor(quarters + 0.5)
    angle = (quarters - whole) * (math.pi / 2.0)
    square = angle * angle
    sine = angle * (1.0 + square * (-1.0 / 6 + square * (1.0 / 120 + square * (-1.0 / 5040))))
    cosine = 1.0 + square * (-0.5 + square * (1.0 / 24 + square * (-1.0 / 720 + square * (1.0 / 40320))))
    quadrant = whole.astype(jnp.int32)
    swapped = (quadrant & 1) != 0
    first = jnp.where(swapped, sine, cosine)
    second = jnp.where(swapped, cosine, sine)
    first = jnp.where(((quadrant + 1) & 2) != 0, -first, first)
    second = jnp.where((quadrant & 2) != 0, -second, second)
    return first, second


def nt_dot(a, b):
    return lax.dot_general(a, b, (((1,), (1,)), ((), ())), preferred_element_type=jnp.float32)


def spectra_kernel(bands, lons, subs, lag, unroll, target_hbm, qu_hbm, off_hbm, rb_hbm, cb_hbm, orders_hbm, out_ref,
                   target_ref, qu_ref, off_ref, rb_ref, cb_ref, orders_ref, keys_row, keys, sums, tiles, halo, order_col, t_hi, t_lo,
                   turn, spin, g_hi, g_lo, part, arrived, total, landed, in_sem, keys_sem, halo_send, halo_recv, x_send, x_recv, a_send, a_recv):
    band = lax.axis_index("band")
    lon = lax.axis_index("lon")
    run = bands // subs
    per_sub = 2 * run
    per_group = per_sub * lons
    per_lon = 2 * bands
    quarter = band // run
    above = lax.rem(band + bands - 1, bands)
    below = lax.rem(band + 1, bands)
    blocks = rb_ref.shape[0]

    arrays = ((target_hbm, target_ref), (cb_hbm, cb_ref), (rb_hbm, rb_ref), (off_hbm, off_ref), (qu_hbm, qu_ref),
              (orders_hbm, orders_ref))
    inputs = [pltpu.make_async_copy(source, here, in_sem.at[i]) for i, (source, here) in enumerate(arrays)]
    for copy in inputs:
        copy.start()

    barrier = pltpu.get_barrier_semaphore()
    for step in range(1, lons):
        pl.semaphore_signal(barrier, inc=1, device_id=(band, lax.rem(lon + step, lons)), device_id_type=MESH)

    inputs[0].wait()
    lane128 = lax.broadcasted_iota(jnp.int32, (1, 128), 1)
    row_keys, col_keys = [], []
    for h in range(blocks // 128):
        row = (target_ref[:, h * 128:h * 128 + 128] * blocks + (lane128 + h * 128)).astype(jnp.float32)
        row_keys.append(row)
        col_keys.append(jnp.transpose(jnp.broadcast_to(row, (128, 128))))
    ranks = []
    for col in col_keys:
        before = jnp.zeros((128, 128), jnp.float32)
        for row in row_keys:
            before = before + jnp.where(row < col, 1.0, 0.0)
        ranks.append(jnp.sum(before, 1, keepdims=True))
    upto = jnp.zeros((1, 128), jnp.float32)
    for col in col_keys:
        limit = ((lane128 + 1) * blocks).astype(jnp.float32)
        upto = upto + jnp.sum(jnp.where(col < limit, 1.0, 0.0), 0, keepdims=True)
    for h in range(blocks // 128):
        place = (lane128 + h * 128).astype(jnp.float32)
        row = jnp.zeros((1, 128), jnp.float32)
        for col, rank in zip(col_keys, ranks):
            row = row + jnp.sum(jnp.where(rank == place, col, 0.0), 0, keepdims=True)
        keys_row[pl.ds(h, 1), :] = row.astype(jnp.int32)
    keys_row[pl.ds(blocks // 128, 1), :] = upto.astype(jnp.int32)
    to_scalars = pltpu.make_async_copy(keys_row, keys, keys_sem)
    to_scalars.start()
    to_scalars.wait()
    for copy in inputs[1:]:
        copy.wait()

    pos = lax.broadcasted_iota(jnp.int32, (TR, 128), 0)

    def block_tile(n):
        row = pl.ds(n, 1)
        cb = cb_ref[row, :]
        col_o = (pos - cb) & 15
        d = col_o.astype(jnp.float32) - (off_ref[1, row, :] + 3.0)
        v_hi, v_lo = split(jnp.exp2(d * d * TAP_SCALE))
        group = jnp.where(col_o < 8, cb + col_o - pos, -16).astype(jnp.bfloat16)
        zero = jnp.zeros((TR, 128), jnp.bfloat16)
        hi, lo = [], []
        for sixteen in range(TC // 16):
            here = group == jnp.bfloat16(16 * sixteen)
            hi.append(jnp.where(here, v_hi, zero))
            lo.append(jnp.where(here, v_lo, zero))
        cols = jnp.concatenate([jnp.concatenate(hi, 0), jnp.concatenate(lo, 0)], 1)
        row_o = (pos - rb_ref[row, :]) & 15
        e = row_o.astype(jnp.float32) - (off_ref[0, row, :] + 3.0)
        a = jnp.where(row_o < 8, jnp.exp2(e * e * TAP_SCALE), 0.0)
        q_hi, q_lo = split(a * qu_ref[0, row, :])
        u_hi, u_lo = split(a * qu_ref[1, row, :])
        half = jnp.concatenate([q_hi, u_hi, q_lo, u_lo], 0)
        out = nt_dot(jnp.concatenate([half, half], 1), cols)
        return out[:2 * TR] + out[2 * TR:]

    greets = bands * unroll // blocks
    key_bits = blocks.bit_length() - 1

    def deposit(i, carry):
        for j in range(greets):
            step = i * greets + j

            @pl.when(step > 0)
            def _():
                pl.semaphore_signal(barrier, inc=1, device_id=(lax.rem(band + step, bands), lon), device_id_type=MESH)

        running, last_tile = carry
        for j in range(unroll):
            place = i * unroll + j
            key = keys[place // 128, place % 128]
            tile = key >> key_bits
            same = jnp.where(tile == last_tile, 1.0, 0.0)
            running = running * same + block_tile(key & (blocks - 1))
            sums[place] = running
            last_tile = tile
        return running, last_tile

    lax.fori_loop(0, blocks // unroll, deposit, (jnp.zeros((2 * TR, TC), jnp.float32), jnp.int32(-1)))

    def gather(tile, carry):
        last = (keys[blocks // 128, tile] - 1) & (blocks - 1)
        found = jnp.where((keys[last >> 7, last & 127] >> key_bits) == tile, 1.0, 0.0)
        tiles[tile] = sums[last] * found
        return carry

    lax.fori_loop(0, 64, gather, 0, unroll=8)
    pl.semaphore_wait(barrier, bands - 1 + lons - 1)

    upward = pltpu.make_async_remote_copy(
        src_ref=tiles.at[pl.ds(0, 16)], dst_ref=halo.at[1], send_sem=halo_send.at[0], recv_sem=halo_recv.at[1],
        device_id=(above, lon), device_id_type=MESH)
    downward = pltpu.make_async_remote_copy(
        src_ref=tiles.at[pl.ds(48, 16)], dst_ref=halo.at[0], send_sem=halo_send.at[1], recv_sem=halo_recv.at[0],
        device_id=(below, lon), device_id_type=MESH)
    upward.start()
    downward.start()

    lane = lax.broadcasted_iota(jnp.int32, (1, 128), 1)
    half = lane // 64
    for row in range(8):
        order_col[pl.ds(row * 128, 128), :] = jnp.transpose(
            jnp.broadcast_to(orders_ref[pl.ds(row, 1), :].astype(jnp.float32), (128, 128)))
    cycle = band * ROWS_DEV + ((lane // 32) % 2) * TR + lane % 16
    _, sine = cos_sin((cycle.astype(jnp.float32) + 0.5) * (1.0 / 2048))
    weight = sine * (math.pi * math.sqrt(2.0 / (bands * ROWS_DEV * NPHI)))
    low_columns = lane.astype(jnp.float32) * (1.0 / 2048)
    spin_phase = (half * 1024 + lon * 2048).astype(jnp.float32) * (1.0 / 2048)

    def table(step, carry):
        group = step // lons
        ell = lax.rem(step, lons)
        first = group * per_group + 2 * ell
        m = jnp.concatenate([order_col[pl.ds(first + place, run, stride=2 * lons), :] for place in range(2)], 0)
        rows = pl.ds(pl.multiple_of(ell * 2 * run, 2 * run), 2 * run)
        sine_rows = pl.ds(pl.multiple_of(per_group + ell * 2 * run, 2 * run), 2 * run)
        for side in range(2):
            c, s = cos_sin(m * (low_columns + side * (128.0 / 2048)))
            c_hi, c_lo = split(c)
            s_hi, s_lo = split(-s)
            cols = pl.ds(side * 128, 128)
            t_hi[group, rows, cols] = c_hi
            t_lo[group, rows, cols] = c_lo
            t_hi[group, sine_rows, cols] = s_hi
            t_lo[group, sine_rows, cols] = s_lo
        c, s = cos_sin(m * (256.0 / 2048))
        turn[group, 0, rows, :] = c
        turn[group, 1, rows, :] = -s
        eighth = (m.astype(jnp.int32) & 7).astype(jnp.float32)
        c, s = cos_sin(eighth * spin_phase)
        spin[group, 0, rows, :] = c * weight
        spin[group, 1, rows, :] = -s * weight
        return carry

    lax.fori_loop(0, subs * lons, table, 0)

    upward.wait_recv()
    downward.wait_recv()

    for v in range(4):
        for k in range(2):
            pieces = []
            for h in range(2):
                for tr in range(2):
                    tile = 2 * (v + 4 * h) + k
                    pieces.append(tiles[16 * (tr + 1) + tile] + halo[tr, tile])
            hi, lo = split(jnp.transpose(jnp.concatenate(pieces, 0)))
            g_hi[pl.ds(k * 128, 128), pl.ds(v * 128, 128)] = hi
            g_lo[pl.ds(k * 128, 128), pl.ds(v * 128, 128)] = lo

    is_real = lane < 64

    def transform(group):
        def product(v):
            cols = pl.ds(v * 128, 256)
            value = (jnp.dot(t_hi[group], g_hi[:, cols], preferred_element_type=jnp.float32)
                     + jnp.dot(t_hi[group], g_lo[:, cols], preferred_element_type=jnp.float32)
                     + jnp.dot(t_lo[group], g_hi[:, cols], preferred_element_type=jnp.float32))
            return value[:per_group], value[per_group:]

        wr = turn[group, 0]
        wi = turn[group, 1]
        re = im = None
        for v in (2, 0):
            c, s = product(v)
            for side in (1, 0):
                c1 = c[:, side * 128:side * 128 + 128]
                s1 = s[:, side * 128:side * 128 + 128]
                re, im = (c1, s1) if re is None else (re * wr - im * wi + c1, re * wi + im * wr + s1)
        pr = spin[group, 0]
        pi = spin[group, 1]
        zr = re * pr - im * pi
        zi = re * pi + im * pr
        zr = zr + pltpu.roll(zr, 64, 1)
        zi = zi + pltpu.roll(zi, 64, 1)
        z = jnp.where(is_real, zr, zi)
        for k in range(per_group // run):
            ell, place = divmod(k, 2)
            part[group, ell, pl.ds(place, run, stride=2), :] = z[k * run:(k + 1) * run]

    def over_lon(step, group, sub):
        ell = lax.rem(lon + step, lons)
        return pltpu.make_async_remote_copy(
            src_ref=part.at[group, ell], dst_ref=arrived.at[group, lons - step],
            send_sem=x_send.at[step, sub], recv_sem=x_recv.at[lons - step, sub],
            device_id=(band, ell), device_id_type=MESH)

    def send_part(sub, carry):
        group = lax.rem(quarter + sub, subs)
        transform(group)
        for step in (2, 1, 3):
            over_lon(step, group, sub).start()
        return carry

    def send_total(sub, carry):
        group = lax.rem(quarter + sub, subs)
        value = part[group, lon]
        for step in range(1, lons):
            over_lon(step, group, sub).wait_recv()
            value = value + arrived[group, lons - step]
        rows = pl.ds(pl.multiple_of(group * per_sub, per_sub), per_sub)
        total[rows, :] = value

        def send_one(step, carry):
            target = group * run + lax.rem(band + step, run)

            @pl.when(target != band)
            def _():
                pltpu.make_async_remote_copy(
                    src_ref=total.at[pl.ds(2 * target, 2), :], dst_ref=landed.at[pl.ds(2 * band, 2), :],
                    send_sem=a_send, recv_sem=a_recv, device_id=(target, lon), device_id_type=MESH).start()
            return carry

        return lax.fori_loop(0, run, send_one, carry)

    def pipeline(sub, carry):
        @pl.when(sub < subs)
        def _():
            send_part(sub, 0)

        @pl.when(sub >= lag)
        def _():
            send_total(sub - lag, 0)
        return carry

    lax.fori_loop(0, subs + lag, pipeline, 0)

    own = pltpu.make_async_copy(total.at[pl.ds(2 * band, 2), :], landed.at[pl.ds(2 * band, 2), :], a_recv)
    own.start()
    pltpu.make_async_copy(landed, landed, a_recv).wait()

    lanes = lax.broadcasted_iota(jnp.int32, (bands // 4, 128), 1)
    for i in range(2):
        for f in range(2):
            for reim in range(2):
                value = jnp.zeros((bands // 4, 128), jnp.float32)
                for q in range(4):
                    x = landed[pl.ds(2 * q + i, bands // 4, stride=8), :]
                    for tr in range(2):
                        source = reim * 4 + tr * 2 + f
                        target = 2 * q + tr
                        moved = x if source == target else pltpu.roll(x, ((target - source) % 8) * 16, 1)
                        value = jnp.where(lanes // 16 == target, moved, value)
                for j in range(bands // 4):
                    out_ref[i, pl.ds(2 * f + reim, 1), pl.ds(j * 128, 128)] = value[j:j + 1, :]

    upward.wait_send()
    downward.wait_send()
    for sub in range(subs):
        for step in range(1, lons):
            over_lon(step, lax.rem(quarter + sub, subs), sub).wait_send()
    others = pl.ds(0, per_lon - 2)
    pltpu.make_async_copy(total.at[others], total.at[others], a_send).wait()


def spectra(targets, qu, off, rb, cb, orders, bands, lons, subs=4, lag=2, unroll=32):
    V = pl.BlockSpec(memory_space=pltpu.VMEM)
    f32, bf16 = jnp.float32, jnp.bfloat16
    blocks = rb.shape[0]
    return pl.pallas_call(
        functools.partial(spectra_kernel, bands, lons, subs, lag, unroll),
        out_shape=jax.ShapeDtypeStruct((2, 4, bands * ROWS_DEV), f32),
        in_specs=[pl.BlockSpec(memory_space=pl.ANY)] * 6,
        out_specs=V,
        scratch_shapes=[
            pltpu.VMEM(targets.shape, jnp.int32),
            pltpu.VMEM(qu.shape, f32),
            pltpu.VMEM(off.shape, f32),
            pltpu.VMEM(rb.shape, jnp.int32),
            pltpu.VMEM(cb.shape, jnp.int32),
            pltpu.VMEM(orders.shape, jnp.int32),
            pltpu.VMEM((8, 128), jnp.int32),
            pltpu.SMEM((8, 128), jnp.int32),
            pltpu.VMEM((blocks, 2 * TR, TC), f32),
            pltpu.VMEM((64, 2 * TR, TC), f32),
            pltpu.VMEM((2, 16, 2 * TR, TC), f32),
            pltpu.VMEM((1024, 128), f32),
            pltpu.VMEM((subs, 512, 256), bf16),
            pltpu.VMEM((subs, 512, 256), bf16),
            pltpu.VMEM((subs, 2, 256, 128), f32),
            pltpu.VMEM((subs, 2, 256, 128), f32),
            pltpu.VMEM((256, 512), bf16),
            pltpu.VMEM((256, 512), bf16),
            pltpu.VMEM((subs, lons, 256 // subs, 128), f32),
            pltpu.VMEM((subs, lons, 256 // subs, 128), f32),
            pltpu.VMEM((256, 128), f32),
            pltpu.VMEM((256, 128), f32),
            pltpu.SemaphoreType.DMA((6,)),
            pltpu.SemaphoreType.DMA,
            pltpu.SemaphoreType.DMA((2,)),
            pltpu.SemaphoreType.DMA((2,)),
            pltpu.SemaphoreType.DMA((lons, subs)),
            pltpu.SemaphoreType.DMA((lons, subs)),
            pltpu.SemaphoreType.DMA,
            pltpu.SemaphoreType.DMA,
        ],
        compiler_params=pltpu.CompilerParams(collective_id=0, has_side_effects=True, vmem_limit_bytes=63 * 1024 * 1024),
    )(targets, qu, off, rb, cb, orders)


def body(qu_values, tap_offsets, row_base, col_base, tile_of_block, m_orders):
    bands = lax.axis_size("band")
    lons = lax.axis_size("lon")
    return spectra(tile_of_block.reshape(1, -1), qu_values, tap_offsets, row_base, col_base, m_orders.reshape(8, 128),
                   bands, lons)


def solution(mesh):
    placed = (
        P(None, ("band", "lon"), None),
        P(None, ("band", "lon"), None),
        P(("band", "lon"), None),
        P(("band", "lon"), None),
        P(("band", "lon")),
        P(),
    )
    return jax.shard_map(
        body, mesh=mesh, in_specs=placed, out_specs=P(("band", "lon"), None, None), check_vma=False
    )
```

```python
import functools, math
import jax, jax.numpy as jnp
from jax import lax
from jax.experimental import pallas as pl
from jax.experimental.pallas import tpu as pltpu
from jax.sharding import PartitionSpec as P

NPHI = 8192
ROWS_DEV = 32
TR, TC = 16, 128
MESH = pl.DeviceIdType.MESH
TAP_SCALE = -math.log2(math.e) / 8.0


def split(x):
    high = x.astype(jnp.bfloat16)
    return high, (x - high.astype(jnp.float32)).astype(jnp.bfloat16)


def cos_sin(quarters):
    whole = jnp.floor(quarters + 0.5)
    angle = (quarters - whole) * (math.pi / 2.0)
    square = angle * angle
    sine = angle * (1.0 + square * (-1.0 / 6 + square * (1.0 / 120 + square * (-1.0 / 5040))))
    cosine = 1.0 + square * (-0.5 + square * (1.0 / 24 + square * (-1.0 / 720 + square * (1.0 / 40320))))
    quadrant = whole.astype(jnp.int32)
    swapped = (quadrant & 1) != 0
    first = jnp.where(swapped, sine, cosine)
    second = jnp.where(swapped, cosine, sine)
    first = jnp.where(((quadrant + 1) & 2) != 0, -first, first)
    second = jnp.where((quadrant & 2) != 0, -second, second)
    return first, second


def nt_dot(a, b):
    return lax.dot_general(a, b, (((1,), (1,)), ((), ())), preferred_element_type=jnp.float32)


def spectra_kernel(bands, lons, subs, lag, unroll, target_hbm, qu_hbm, off_hbm, rb_hbm, cb_hbm, orders_hbm, out_ref,
                   target_ref, qu_ref, off_ref, rb_ref, cb_ref, orders_ref, keys_row, keys, sums, tiles, halo, order_col, t_hi, t_lo,
                   turn, spin, g_hi, g_lo, part, arrived, total, landed, ready, in_sem, keys_sem, halo_send, halo_recv, x_send, x_recv, a_send, a_recv):
    band = lax.axis_index("band")
    lon = lax.axis_index("lon")
    run = bands // subs
    per_sub = 2 * run
    per_group = per_sub * lons
    per_lon = 2 * bands
    quarter = band // run
    above = lax.rem(band + bands - 1, bands)
    below = lax.rem(band + 1, bands)
    blocks = rb_ref.shape[0]

    arrays = ((target_hbm, target_ref), (cb_hbm, cb_ref), (rb_hbm, rb_ref), (off_hbm, off_ref), (qu_hbm, qu_ref),
              (orders_hbm, orders_ref))
    inputs = [pltpu.make_async_copy(source, here, in_sem.at[i]) for i, (source, here) in enumerate(arrays)]
    for copy in inputs:
        copy.start()

    width = bands // 8
    first_of_row = band // width * width

    def in_row(step):
        return first_of_row + lax.rem(band + step, width)

    barrier = pltpu.get_barrier_semaphore()
    greeted = [(above, lon), (below, lon)]
    greeted += [(band, lax.rem(lon + step, lons)) for step in range(1, lons)]
    greeted += [(in_row(step), lon) for step in range(1, width)]
    greeted += [(lax.rem(band + step * width, bands), lon) for step in range(1, bands // width)]
    for place in greeted:
        pl.semaphore_signal(barrier, inc=1, device_id=place, device_id_type=MESH)

    inputs[0].wait()
    lane128 = lax.broadcasted_iota(jnp.int32, (1, 128), 1)
    row_keys, col_keys = [], []
    for h in range(blocks // 128):
        row = (target_ref[:, h * 128:h * 128 + 128] * blocks + (lane128 + h * 128)).astype(jnp.float32)
        row_keys.append(row)
        col_keys.append(jnp.transpose(jnp.broadcast_to(row, (128, 128))))
    ranks = []
    for col in col_keys:
        before = jnp.zeros((128, 128), jnp.float32)
        for row in row_keys:
            before = before + jnp.where(row < col, 1.0, 0.0)
        ranks.append(jnp.sum(before, 1, keepdims=True))
    upto = jnp.zeros((1, 128), jnp.float32)
    for col in col_keys:
        limit = ((lane128 + 1) * blocks).astype(jnp.float32)
        upto = upto + jnp.sum(jnp.where(col < limit, 1.0, 0.0), 0, keepdims=True)
    for h in range(blocks // 128):
        place = (lane128 + h * 128).astype(jnp.float32)
        row = jnp.zeros((1, 128), jnp.float32)
        for col, rank in zip(col_keys, ranks):
            row = row + jnp.sum(jnp.where(rank == place, col, 0.0), 0, keepdims=True)
        keys_row[pl.ds(h, 1), :] = row.astype(jnp.int32)
    keys_row[pl.ds(blocks // 128, 1), :] = upto.astype(jnp.int32)
    to_scalars = pltpu.make_async_copy(keys_row, keys, keys_sem)
    to_scalars.start()
    to_scalars.wait()
    for copy in inputs[1:]:
        copy.wait()

    pos = lax.broadcasted_iota(jnp.int32, (TR, 128), 0)

    def block_tile(n):
        row = pl.ds(n, 1)
        cb = cb_ref[row, :]
        col_o = (pos - cb) & 15
        d = col_o.astype(jnp.float32) - (off_ref[1, row, :] + 3.0)
        v_hi, v_lo = split(jnp.exp2(d * d * TAP_SCALE))
        group = jnp.where(col_o < 8, cb + col_o - pos, -16).astype(jnp.bfloat16)
        zero = jnp.zeros((TR, 128), jnp.bfloat16)
        hi, lo = [], []
        for sixteen in range(TC // 16):
            here = group == jnp.bfloat16(16 * sixteen)
            hi.append(jnp.where(here, v_hi, zero))
            lo.append(jnp.where(here, v_lo, zero))
        cols = jnp.concatenate([jnp.concatenate(hi, 0), jnp.concatenate(lo, 0)], 1)
        row_o = (pos - rb_ref[row, :]) & 15
        e = row_o.astype(jnp.float32) - (off_ref[0, row, :] + 3.0)
        a = jnp.where(row_o < 8, jnp.exp2(e * e * TAP_SCALE), 0.0)
        q_hi, q_lo = split(a * qu_ref[0, row, :])
        u_hi, u_lo = split(a * qu_ref[1, row, :])
        half = jnp.concatenate([q_hi, u_hi, q_lo, u_lo], 0)
        out = nt_dot(jnp.concatenate([half, half], 1), cols)
        return out[:2 * TR] + out[2 * TR:]

    key_bits = blocks.bit_length() - 1

    def deposit(i, carry):
        running, last_tile = carry
        for j in range(unroll):
            place = i * unroll + j
            key = keys[place // 128, place % 128]
            tile = key >> key_bits
            same = jnp.where(tile == last_tile, 1.0, 0.0)
            running = running * same + block_tile(key & (blocks - 1))
            sums[place] = running
            last_tile = tile
        return running, last_tile

    lax.fori_loop(0, blocks // unroll, deposit, (jnp.zeros((2 * TR, TC), jnp.float32), jnp.int32(-1)))

    def gather(tile, carry):
        last = (keys[blocks // 128, tile] - 1) & (blocks - 1)
        found = jnp.where((keys[last >> 7, last & 127] >> key_bits) == tile, 1.0, 0.0)
        tiles[tile] = sums[last] * found
        return carry

    lax.fori_loop(0, 64, gather, 0, unroll=8)
    pl.semaphore_wait(barrier, len(greeted))

    upward = pltpu.make_async_remote_copy(
        src_ref=tiles.at[pl.ds(0, 16)], dst_ref=halo.at[1], send_sem=halo_send.at[0], recv_sem=halo_recv.at[1],
        device_id=(above, lon), device_id_type=MESH)
    downward = pltpu.make_async_remote_copy(
        src_ref=tiles.at[pl.ds(48, 16)], dst_ref=halo.at[0], send_sem=halo_send.at[1], recv_sem=halo_recv.at[0],
        device_id=(below, lon), device_id_type=MESH)
    upward.start()
    downward.start()
    for step in range(1, width):
        pl.semaphore_signal(ready, inc=1, device_id=(in_row(step), lon), device_id_type=MESH)

    lane = lax.broadcasted_iota(jnp.int32, (1, 128), 1)
    half = lane // 64
    for row in range(8):
        order_col[pl.ds(row * 128, 128), :] = jnp.transpose(
            jnp.broadcast_to(orders_ref[pl.ds(row, 1), :].astype(jnp.float32), (128, 128)))
    cycle = band * ROWS_DEV + ((lane // 32) % 2) * TR + lane % 16
    _, sine = cos_sin((cycle.astype(jnp.float32) + 0.5) * (1.0 / 2048))
    weight = sine * (math.pi * math.sqrt(2.0 / (bands * ROWS_DEV * NPHI)))
    low_columns = lane.astype(jnp.float32) * (1.0 / 2048)
    spin_phase = (half * 1024 + lon * 2048).astype(jnp.float32) * (1.0 / 2048)

    def table(step, carry):
        group = step // lons
        ell = lax.rem(step, lons)
        first = group * per_group + 2 * ell
        m = jnp.concatenate([order_col[pl.ds(first + place, run, stride=2 * lons), :] for place in range(2)], 0)
        rows = pl.ds(pl.multiple_of(ell * 2 * run, 2 * run), 2 * run)
        sine_rows = pl.ds(pl.multiple_of(per_group + ell * 2 * run, 2 * run), 2 * run)
        for side in range(2):
            c, s = cos_sin(m * (low_columns + side * (128.0 / 2048)))
            c_hi, c_lo = split(c)
            s_hi, s_lo = split(-s)
            cols = pl.ds(side * 128, 128)
            t_hi[group, rows, cols] = c_hi
            t_lo[group, rows, cols] = c_lo
            t_hi[group, sine_rows, cols] = s_hi
            t_lo[group, sine_rows, cols] = s_lo
        c, s = cos_sin(m * (256.0 / 2048))
        turn[group, 0, rows, :] = c
        turn[group, 1, rows, :] = -s
        eighth = (m.astype(jnp.int32) & 7).astype(jnp.float32)
        c, s = cos_sin(eighth * spin_phase)
        spin[group, 0, rows, :] = c * weight
        spin[group, 1, rows, :] = -s * weight
        return carry

    lax.fori_loop(0, subs * lons, table, 0)

    upward.wait_recv()
    downward.wait_recv()

    for v in range(4):
        for k in range(2):
            pieces = []
            for h in range(2):
                for tr in range(2):
                    tile = 2 * (v + 4 * h) + k
                    pieces.append(tiles[16 * (tr + 1) + tile] + halo[tr, tile])
            hi, lo = split(jnp.transpose(jnp.concatenate(pieces, 0)))
            g_hi[pl.ds(k * 128, 128), pl.ds(v * 128, 128)] = hi
            g_lo[pl.ds(k * 128, 128), pl.ds(v * 128, 128)] = lo

    is_real = lane < 64

    def transform(group):
        def product(v):
            cols = pl.ds(v * 128, 256)
            value = (jnp.dot(t_hi[group], g_hi[:, cols], preferred_element_type=jnp.float32)
                     + jnp.dot(t_hi[group], g_lo[:, cols], preferred_element_type=jnp.float32)
                     + jnp.dot(t_lo[group], g_hi[:, cols], preferred_element_type=jnp.float32))
            return value[:per_group], value[per_group:]

        wr = turn[group, 0]
        wi = turn[group, 1]
        re = im = None
        for v in (2, 0):
            c, s = product(v)
            for side in (1, 0):
                c1 = c[:, side * 128:side * 128 + 128]
                s1 = s[:, side * 128:side * 128 + 128]
                re, im = (c1, s1) if re is None else (re * wr - im * wi + c1, re * wi + im * wr + s1)
        pr = spin[group, 0]
        pi = spin[group, 1]
        zr = re * pr - im * pi
        zi = re * pi + im * pr
        zr = zr + pltpu.roll(zr, 64, 1)
        zi = zi + pltpu.roll(zi, 64, 1)
        z = jnp.where(is_real, zr, zi)
        for k in range(per_group // run):
            ell, place = divmod(k, 2)
            part[group, ell, pl.ds(place, run, stride=2), :] = z[k * run:(k + 1) * run]

    def over_lon(step, group, sub):
        ell = lax.rem(lon + step, lons)
        return pltpu.make_async_remote_copy(
            src_ref=part.at[group, ell], dst_ref=arrived.at[group, lons - step],
            send_sem=x_send.at[step, sub], recv_sem=x_recv.at[lons - step, sub],
            device_id=(band, ell), device_id_type=MESH)

    def far(step):
        return -min(step // 2 % 8, 8 - step // 2 % 8)

    def group_of(sub):
        ahead = jnp.int32(0)
        for i, step in enumerate(sorted(range(1, subs), key=lambda step: -min(step, subs - step))):
            ahead = jnp.where(sub == i, step, ahead)
        return lax.rem(quarter + ahead, subs)

    def send_part(sub, carry):
        group = group_of(sub)
        transform(group)
        for step in (2, 1, 3):
            over_lon(step, group, sub).start()
        return carry

    def send_total(sub, carry):
        group = group_of(sub)
        value = part[group, lon]
        for step in range(1, lons):
            over_lon(step, group, sub).wait_recv()
            value = value + arrived[group, lons - step]
        rows = pl.ds(pl.multiple_of(group * per_sub, per_sub), per_sub)
        total[rows, :] = value

        def send_one(target):
            pltpu.make_async_remote_copy(
                src_ref=total.at[pl.ds(2 * target, 2), :], dst_ref=landed.at[pl.ds(2 * band, 2), :],
                send_sem=a_send, recv_sem=a_recv, device_id=(target, lon), device_id_type=MESH).start()

        for step in sorted(range(1, run), key=far):
            send_one(group * run + lax.rem(band + step, run))

        @pl.when(group != quarter)
        def _():
            send_one(group * run + lax.rem(band, run))
        return carry

    def pipeline(sub, carry):
        @pl.when(sub < subs)
        def _():
            send_part(sub, 0)

        @pl.when(sub == lag)
        def _():
            pl.semaphore_wait(ready, width - 1)

        @pl.when(sub >= lag)
        def _():
            send_total(sub - lag, 0)
        return carry

    lax.fori_loop(0, subs + lag, pipeline, 0)

    own = pltpu.make_async_copy(total.at[pl.ds(2 * band, 2), :], landed.at[pl.ds(2 * band, 2), :], a_recv)
    own.start()
    pltpu.make_async_copy(landed, landed, a_recv).wait()

    lanes = lax.broadcasted_iota(jnp.int32, (bands // 4, 128), 1)
    for i in range(2):
        for f in range(2):
            for reim in range(2):
                value = jnp.zeros((bands // 4, 128), jnp.float32)
                for q in range(4):
                    x = landed[pl.ds(2 * q + i, bands // 4, stride=8), :]
                    for tr in range(2):
                        source = reim * 4 + tr * 2 + f
                        target = 2 * q + tr
                        moved = x if source == target else pltpu.roll(x, ((target - source) % 8) * 16, 1)
                        value = jnp.where(lanes // 16 == target, moved, value)
                for j in range(bands // 4):
                    out_ref[i, pl.ds(2 * f + reim, 1), pl.ds(j * 128, 128)] = value[j:j + 1, :]

    upward.wait_send()
    downward.wait_send()
    for sub in range(subs):
        for step in range(1, lons):
            over_lon(step, group_of(sub), sub).wait_send()
    others = pl.ds(0, per_lon - 2)
    pltpu.make_async_copy(total.at[others], total.at[others], a_send).wait()


def spectra(targets, qu, off, rb, cb, orders, bands, lons, subs=4, lag=3, unroll=32):
    V = pl.BlockSpec(memory_space=pltpu.VMEM)
    f32, bf16 = jnp.float32, jnp.bfloat16
    blocks = rb.shape[0]
    return pl.pallas_call(
        functools.partial(spectra_kernel, bands, lons, subs, lag, unroll),
        out_shape=jax.ShapeDtypeStruct((2, 4, bands * ROWS_DEV), f32),
        in_specs=[pl.BlockSpec(memory_space=pl.ANY)] * 6,
        out_specs=V,
        scratch_shapes=[
            pltpu.VMEM(targets.shape, jnp.int32),
            pltpu.VMEM(qu.shape, f32),
            pltpu.VMEM(off.shape, f32),
            pltpu.VMEM(rb.shape, jnp.int32),
            pltpu.VMEM(cb.shape, jnp.int32),
            pltpu.VMEM(orders.shape, jnp.int32),
            pltpu.VMEM((8, 128), jnp.int32),
            pltpu.SMEM((8, 128), jnp.int32),
            pltpu.VMEM((blocks, 2 * TR, TC), f32),
            pltpu.VMEM((64, 2 * TR, TC), f32),
            pltpu.VMEM((2, 16, 2 * TR, TC), f32),
            pltpu.VMEM((1024, 128), f32),
            pltpu.VMEM((subs, 512, 256), bf16),
            pltpu.VMEM((subs, 512, 256), bf16),
            pltpu.VMEM((subs, 2, 256, 128), f32),
            pltpu.VMEM((subs, 2, 256, 128), f32),
            pltpu.VMEM((256, 512), bf16),
            pltpu.VMEM((256, 512), bf16),
            pltpu.VMEM((subs, lons, 256 // subs, 128), f32),
            pltpu.VMEM((subs, lons, 256 // subs, 128), f32),
            pltpu.VMEM((256, 128), f32),
            pltpu.VMEM((256, 128), f32),
            pltpu.SemaphoreType.REGULAR,
            pltpu.SemaphoreType.DMA((6,)),
            pltpu.SemaphoreType.DMA,
            pltpu.SemaphoreType.DMA((2,)),
            pltpu.SemaphoreType.DMA((2,)),
            pltpu.SemaphoreType.DMA((lons, subs)),
            pltpu.SemaphoreType.DMA((lons, subs)),
            pltpu.SemaphoreType.DMA,
            pltpu.SemaphoreType.DMA,
        ],
        compiler_params=pltpu.CompilerParams(collective_id=0, has_side_effects=True, vmem_limit_bytes=63 * 1024 * 1024),
    )(targets, qu, off, rb, cb, orders)


def body(qu_values, tap_offsets, row_base, col_base, tile_of_block, m_orders):
    bands = lax.axis_size("band")
    lons = lax.axis_size("lon")
    return spectra(tile_of_block.reshape(1, -1), qu_values, tap_offsets, row_base, col_base, m_orders.reshape(8, 128),
                   bands, lons)


def solution(mesh):
    placed = (
        P(None, ("band", "lon"), None),
        P(None, ("band", "lon"), None),
        P(("band", "lon"), None),
        P(("band", "lon"), None),
        P(("band", "lon")),
        P(),
    )
    return jax.shard_map(
        body, mesh=mesh, in_specs=placed, out_specs=P(("band", "lon"), None, None), check_vma=False
    )
```

```python
import functools, math
import jax, jax.numpy as jnp
from jax import lax
from jax.experimental import pallas as pl
from jax.experimental.pallas import tpu as pltpu
from jax.sharding import PartitionSpec as P

NPHI = 8192
ROWS_DEV = 32
TR, TC = 16, 128
MESH = pl.DeviceIdType.MESH
TAP_SCALE = -math.log2(math.e) / 8.0


def split(x):
    high = x.astype(jnp.bfloat16)
    return high, (x - high.astype(jnp.float32)).astype(jnp.bfloat16)


def cos_sin(quarters):
    whole = jnp.floor(quarters + 0.5)
    angle = (quarters - whole) * (math.pi / 2.0)
    square = angle * angle
    sine = angle * (1.0 + square * (-1.0 / 6 + square * (1.0 / 120 + square * (-1.0 / 5040))))
    cosine = 1.0 + square * (-0.5 + square * (1.0 / 24 + square * (-1.0 / 720 + square * (1.0 / 40320))))
    quadrant = whole.astype(jnp.int32)
    swapped = (quadrant & 1) != 0
    first = jnp.where(swapped, sine, cosine)
    second = jnp.where(swapped, cosine, sine)
    first = jnp.where(((quadrant + 1) & 2) != 0, -first, first)
    second = jnp.where((quadrant & 2) != 0, -second, second)
    return first, second


def nt_dot(a, b):
    return lax.dot_general(a, b, (((1,), (1,)), ((), ())), preferred_element_type=jnp.float32)


def spectra_kernel(bands, lons, subs, lag, unroll, target_hbm, qu_hbm, off_hbm, rb_hbm, cb_hbm, orders_hbm, out_ref,
                   target_ref, qu_ref, off_ref, rb_ref, cb_ref, orders_ref, keys_row, keys, sums, tiles, halo, order_col, t_hi, t_lo,
                   turn, spin, g_hi, g_lo, part, arrived, total, landed, ready, in_sem, keys_sem, halo_send, halo_recv, x_send, x_recv, a_send, a_recv):
    band = lax.axis_index("band")
    lon = lax.axis_index("lon")
    run = bands // subs
    per_sub = 2 * run
    per_group = per_sub * lons
    per_lon = 2 * bands
    quarter = band // run
    above = lax.rem(band + bands - 1, bands)
    below = lax.rem(band + 1, bands)
    blocks = rb_ref.shape[0]

    arrays = ((target_hbm, target_ref), (cb_hbm, cb_ref), (rb_hbm, rb_ref), (off_hbm, off_ref), (qu_hbm, qu_ref),
              (orders_hbm, orders_ref))
    inputs = [pltpu.make_async_copy(source, here, in_sem.at[i]) for i, (source, here) in enumerate(arrays)]
    for copy in inputs:
        copy.start()

    width = bands // 8
    first_of_row = band // width * width

    def in_row(step):
        return first_of_row + lax.rem(band + step, width)

    barrier = pltpu.get_barrier_semaphore()
    greeted = [(above, lon), (below, lon)]
    greeted += [(band, lax.rem(lon + step, lons)) for step in range(1, lons)]
    greeted += [(in_row(step), lon) for step in range(1, width)]
    greeted += [(lax.rem(band + step * width, bands), lon) for step in range(1, bands // width)]
    for place in greeted:
        pl.semaphore_signal(barrier, inc=1, device_id=place, device_id_type=MESH)

    inputs[0].wait()
    lane128 = lax.broadcasted_iota(jnp.int32, (1, 128), 1)
    row_keys, col_keys = [], []
    for h in range(blocks // 128):
        row = (target_ref[:, h * 128:h * 128 + 128] * blocks + (lane128 + h * 128)).astype(jnp.float32)
        row_keys.append(row)
        col_keys.append(jnp.transpose(jnp.broadcast_to(row, (128, 128))))
    ranks = []
    for col in col_keys:
        before = jnp.zeros((128, 128), jnp.float32)
        for row in row_keys:
            before = before + jnp.where(row < col, 1.0, 0.0)
        ranks.append(jnp.sum(before, 1, keepdims=True))
    through = jnp.zeros((1, 128), jnp.float32)
    ahead = jnp.zeros((1, 128), jnp.float32)
    first_key = (lane128 * blocks).astype(jnp.float32)
    for col in col_keys:
        ahead = ahead + jnp.sum(jnp.where(col < first_key, 1.0, 0.0), 0, keepdims=True)
        through = through + jnp.sum(jnp.where(col < first_key + blocks, 1.0, 0.0), 0, keepdims=True)
    last_place = jnp.where(through > ahead, through - 1.0, float(blocks))
    for h in range(blocks // 128):
        place = (lane128 + h * 128).astype(jnp.float32)
        row = jnp.zeros((1, 128), jnp.float32)
        for col, rank in zip(col_keys, ranks):
            row = row + jnp.sum(jnp.where(rank == place, col, 0.0), 0, keepdims=True)
        keys_row[pl.ds(h, 1), :] = row.astype(jnp.int32)
    keys_row[pl.ds(blocks // 128, 1), :] = last_place.astype(jnp.int32)
    sums[blocks] = jnp.zeros((2 * TR, TC), jnp.float32)
    to_scalars = pltpu.make_async_copy(keys_row, keys, keys_sem)
    to_scalars.start()
    to_scalars.wait()
    for copy in inputs[1:]:
        copy.wait()

    pos = lax.broadcasted_iota(jnp.int32, (TR, 128), 0)

    def block_tile(n):
        row = pl.ds(n, 1)
        cb = cb_ref[row, :]
        col_o = (pos - cb) & 15
        d = col_o.astype(jnp.float32) - (off_ref[1, row, :] + 3.0)
        v_hi, v_lo = split(jnp.exp2(d * d * TAP_SCALE))
        group = jnp.where(col_o < 8, cb + col_o - pos, -16).astype(jnp.bfloat16)
        zero = jnp.zeros((TR, 128), jnp.bfloat16)
        hi, lo = [], []
        for sixteen in range(TC // 16):
            here = group == jnp.bfloat16(16 * sixteen)
            hi.append(jnp.where(here, v_hi, zero))
            lo.append(jnp.where(here, v_lo, zero))
        cols = jnp.concatenate([jnp.concatenate(hi, 0), jnp.concatenate(lo, 0)], 1)
        row_o = (pos - rb_ref[row, :]) & 15
        e = row_o.astype(jnp.float32) - (off_ref[0, row, :] + 3.0)
        a = jnp.where(row_o < 8, jnp.exp2(e * e * TAP_SCALE), 0.0)
        q_hi, q_lo = split(a * qu_ref[0, row, :])
        u_hi, u_lo = split(a * qu_ref[1, row, :])
        half = jnp.concatenate([q_hi, u_hi, q_lo, u_lo], 0)
        out = jnp.transpose(nt_dot(cols, jnp.concatenate([half, half], 1)))
        return out[:2 * TR] + out[2 * TR:]

    key_bits = blocks.bit_length() - 1

    def deposit(i, carry):
        running, last_tile = carry
        for j in range(unroll):
            place = i * unroll + j
            key = keys[place // 128, place % 128]
            tile = key >> key_bits
            same = jnp.where(tile == last_tile, 1.0, 0.0)
            running = running * same + block_tile(key & (blocks - 1))
            sums[place] = running
            last_tile = tile
        return running, last_tile

    lax.fori_loop(0, blocks // unroll, deposit, (jnp.zeros((2 * TR, TC), jnp.float32), jnp.int32(-1)))

    def gather(tile, carry):
        tiles[tile] = sums[jnp.clip(keys[blocks // 128, tile], 0, blocks)]
        return carry

    lax.fori_loop(0, 16, gather, 0, unroll=16)
    lax.fori_loop(48, 64, gather, 0, unroll=16)
    pl.semaphore_wait(barrier, len(greeted))

    upward = pltpu.make_async_remote_copy(
        src_ref=tiles.at[pl.ds(0, 16)], dst_ref=halo.at[1], send_sem=halo_send.at[0], recv_sem=halo_recv.at[1],
        device_id=(above, lon), device_id_type=MESH)
    downward = pltpu.make_async_remote_copy(
        src_ref=tiles.at[pl.ds(48, 16)], dst_ref=halo.at[0], send_sem=halo_send.at[1], recv_sem=halo_recv.at[0],
        device_id=(below, lon), device_id_type=MESH)
    upward.start()
    downward.start()
    for step in range(1, width):
        pl.semaphore_signal(ready, inc=1, device_id=(in_row(step), lon), device_id_type=MESH)

    lax.fori_loop(16, 48, gather, 0, unroll=16)

    lane = lax.broadcasted_iota(jnp.int32, (1, 128), 1)
    half = lane // 64
    for row in range(8):
        order_col[pl.ds(row * 128, 128), :] = jnp.transpose(
            jnp.broadcast_to(orders_ref[pl.ds(row, 1), :].astype(jnp.float32), (128, 128)))
    cycle = band * ROWS_DEV + ((lane // 32) % 2) * TR + lane % 16
    _, sine = cos_sin((cycle.astype(jnp.float32) + 0.5) * (1.0 / 2048))
    weight = sine * (math.pi * math.sqrt(2.0 / (bands * ROWS_DEV * NPHI)))
    low_columns = lane.astype(jnp.float32) * (1.0 / 2048)
    spin_phase = (half * 1024 + lon * 2048).astype(jnp.float32) * (1.0 / 2048)

    def table(step, carry):
        group = step // lons
        ell = lax.rem(step, lons)
        first = group * per_group + 2 * ell
        m = jnp.concatenate([order_col[pl.ds(first + place, run, stride=2 * lons), :] for place in range(2)], 0)
        rows = pl.ds(pl.multiple_of(ell * 2 * run, 2 * run), 2 * run)
        sine_rows = pl.ds(pl.multiple_of(per_group + ell * 2 * run, 2 * run), 2 * run)
        for side in range(2):
            c, s = cos_sin(m * (low_columns + side * (128.0 / 2048)))
            c_hi, c_lo = split(c)
            s_hi, s_lo = split(-s)
            cols = pl.ds(side * 128, 128)
            t_hi[group, rows, cols] = c_hi
            t_lo[group, rows, cols] = c_lo
            t_hi[group, sine_rows, cols] = s_hi
            t_lo[group, sine_rows, cols] = s_lo
        c, s = cos_sin(m * (256.0 / 2048))
        turn[group, 0, rows, :] = c
        turn[group, 1, rows, :] = -s
        eighth = (m.astype(jnp.int32) & 7).astype(jnp.float32)
        c, s = cos_sin(eighth * spin_phase)
        spin[group, 0, rows, :] = c * weight
        spin[group, 1, rows, :] = -s * weight
        return carry

    lax.fori_loop(0, subs * lons, table, 0)

    upward.wait_recv()
    downward.wait_recv()

    for v in range(4):
        for k in range(2):
            pieces = []
            for h in range(2):
                for tr in range(2):
                    tile = 2 * (v + 4 * h) + k
                    pieces.append(tiles[16 * (tr + 1) + tile] + halo[tr, tile])
            hi, lo = split(jnp.transpose(jnp.concatenate(pieces, 0)))
            g_hi[pl.ds(k * 128, 128), pl.ds(v * 128, 128)] = hi
            g_lo[pl.ds(k * 128, 128), pl.ds(v * 128, 128)] = lo

    is_real = lane < 64

    def transform(group):
        def product(v):
            cols = pl.ds(v * 128, 256)
            value = (jnp.dot(t_hi[group], g_hi[:, cols], preferred_element_type=jnp.float32)
                     + jnp.dot(t_hi[group], g_lo[:, cols], preferred_element_type=jnp.float32)
                     + jnp.dot(t_lo[group], g_hi[:, cols], preferred_element_type=jnp.float32))
            return value[:per_group], value[per_group:]

        wr = turn[group, 0]
        wi = turn[group, 1]
        re = im = None
        for v in (2, 0):
            c, s = product(v)
            for side in (1, 0):
                c1 = c[:, side * 128:side * 128 + 128]
                s1 = s[:, side * 128:side * 128 + 128]
                re, im = (c1, s1) if re is None else (re * wr - im * wi + c1, re * wi + im * wr + s1)
        pr = spin[group, 0]
        pi = spin[group, 1]
        zr = re * pr - im * pi
        zi = re * pi + im * pr
        zr = zr + pltpu.roll(zr, 64, 1)
        zi = zi + pltpu.roll(zi, 64, 1)
        z = jnp.where(is_real, zr, zi)
        for k in range(per_group // run):
            ell, place = divmod(k, 2)
            part[group, ell, pl.ds(place, run, stride=2), :] = z[k * run:(k + 1) * run]

    def over_lon(step, group, sub):
        ell = lax.rem(lon + step, lons)
        return pltpu.make_async_remote_copy(
            src_ref=part.at[group, ell], dst_ref=arrived.at[group, lons - step],
            send_sem=x_send.at[step, sub], recv_sem=x_recv.at[lons - step, sub],
            device_id=(band, ell), device_id_type=MESH)

    def far(step):
        return -min(step // 2 % 8, 8 - step // 2 % 8)

    def group_of(sub):
        ahead = jnp.int32(0)
        for i, step in enumerate(sorted(range(1, subs), key=lambda step: -min(step, subs - step))):
            ahead = jnp.where(sub == i, step, ahead)
        return lax.rem(quarter + ahead, subs)

    def send_part(sub, carry):
        group = group_of(sub)
        transform(group)
        for step in (2, 1, 3):
            over_lon(step, group, sub).start()
        return carry

    def send_total(sub, carry):
        group = group_of(sub)
        value = part[group, lon]
        for step in range(1, lons):
            over_lon(step, group, sub).wait_recv()
            value = value + arrived[group, lons - step]
        rows = pl.ds(pl.multiple_of(group * per_sub, per_sub), per_sub)
        total[rows, :] = value

        def send_one(target):
            pltpu.make_async_remote_copy(
                src_ref=total.at[pl.ds(2 * target, 2), :], dst_ref=landed.at[pl.ds(2 * band, 2), :],
                send_sem=a_send, recv_sem=a_recv, device_id=(target, lon), device_id_type=MESH).start()

        for step in sorted(range(1, run), key=far):
            send_one(group * run + lax.rem(band + step, run))

        @pl.when(group != quarter)
        def _():
            send_one(group * run + lax.rem(band, run))
        return carry

    def pipeline(sub, carry):
        @pl.when(sub < subs)
        def _():
            send_part(sub, 0)

        @pl.when(sub == lag)
        def _():
            pl.semaphore_wait(ready, width - 1)

        @pl.when(sub >= lag)
        def _():
            send_total(sub - lag, 0)
        return carry

    lax.fori_loop(0, subs + lag, pipeline, 0)

    own = pltpu.make_async_copy(total.at[pl.ds(2 * band, 2), :], landed.at[pl.ds(2 * band, 2), :], a_recv)
    own.start()
    pltpu.make_async_copy(landed, landed, a_recv).wait()

    lanes = lax.broadcasted_iota(jnp.int32, (bands // 4, 128), 1)
    for i in range(2):
        for f in range(2):
            for reim in range(2):
                value = jnp.zeros((bands // 4, 128), jnp.float32)
                for q in range(4):
                    x = landed[pl.ds(2 * q + i, bands // 4, stride=8), :]
                    for tr in range(2):
                        source = reim * 4 + tr * 2 + f
                        target = 2 * q + tr
                        moved = x if source == target else pltpu.roll(x, ((target - source) % 8) * 16, 1)
                        value = jnp.where(lanes // 16 == target, moved, value)
                for j in range(bands // 4):
                    out_ref[i, pl.ds(2 * f + reim, 1), pl.ds(j * 128, 128)] = value[j:j + 1, :]

    upward.wait_send()
    downward.wait_send()
    for sub in range(subs):
        for step in range(1, lons):
            over_lon(step, group_of(sub), sub).wait_send()
    others = pl.ds(0, per_lon - 2)
    pltpu.make_async_copy(total.at[others], total.at[others], a_send).wait()


def spectra(targets, qu, off, rb, cb, orders, bands, lons, subs=4, lag=3, unroll=64):
    V = pl.BlockSpec(memory_space=pltpu.VMEM)
    f32, bf16 = jnp.float32, jnp.bfloat16
    blocks = rb.shape[0]
    return pl.pallas_call(
        functools.partial(spectra_kernel, bands, lons, subs, lag, unroll),
        out_shape=jax.ShapeDtypeStruct((2, 4, bands * ROWS_DEV), f32),
        in_specs=[pl.BlockSpec(memory_space=pl.ANY)] * 6,
        out_specs=V,
        scratch_shapes=[
            pltpu.VMEM(targets.shape, jnp.int32),
            pltpu.VMEM(qu.shape, f32),
            pltpu.VMEM(off.shape, f32),
            pltpu.VMEM(rb.shape, jnp.int32),
            pltpu.VMEM(cb.shape, jnp.int32),
            pltpu.VMEM(orders.shape, jnp.int32),
            pltpu.VMEM((8, 128), jnp.int32),
            pltpu.SMEM((8, 128), jnp.int32),
            pltpu.VMEM((blocks + 1, 2 * TR, TC), f32),
            pltpu.VMEM((64, 2 * TR, TC), f32),
            pltpu.VMEM((2, 16, 2 * TR, TC), f32),
            pltpu.VMEM((1024, 128), f32),
            pltpu.VMEM((subs, 512, 256), bf16),
            pltpu.VMEM((subs, 512, 256), bf16),
            pltpu.VMEM((subs, 2, 256, 128), f32),
            pltpu.VMEM((subs, 2, 256, 128), f32),
            pltpu.VMEM((256, 512), bf16),
            pltpu.VMEM((256, 512), bf16),
            pltpu.VMEM((subs, lons, 256 // subs, 128), f32),
            pltpu.VMEM((subs, lons, 256 // subs, 128), f32),
            pltpu.VMEM((256, 128), f32),
            pltpu.VMEM((256, 128), f32),
            pltpu.SemaphoreType.REGULAR,
            pltpu.SemaphoreType.DMA((6,)),
            pltpu.SemaphoreType.DMA,
            pltpu.SemaphoreType.DMA((2,)),
            pltpu.SemaphoreType.DMA((2,)),
            pltpu.SemaphoreType.DMA((lons, subs)),
            pltpu.SemaphoreType.DMA((lons, subs)),
            pltpu.SemaphoreType.DMA,
            pltpu.SemaphoreType.DMA,
        ],
        compiler_params=pltpu.CompilerParams(collective_id=0, has_side_effects=True, vmem_limit_bytes=63 * 1024 * 1024),
    )(targets, qu, off, rb, cb, orders)


def body(qu_values, tap_offsets, row_base, col_base, tile_of_block, m_orders):
    bands = lax.axis_size("band")
    lons = lax.axis_size("lon")
    return spectra(tile_of_block.reshape(1, -1), qu_values, tap_offsets, row_base, col_base, m_orders.reshape(8, 128),
                   bands, lons)


def solution(mesh):
    placed = (
        P(None, ("band", "lon"), None),
        P(None, ("band", "lon"), None),
        P(("band", "lon"), None),
        P(("band", "lon"), None),
        P(("band", "lon")),
        P(),
    )
    return jax.shard_map(
        body, mesh=mesh, in_specs=placed, out_specs=P(("band", "lon"), None, None), check_vma=False
    )
```

```python
import functools, math
import jax, jax.numpy as jnp
from jax import lax
from jax.experimental import pallas as pl
from jax.experimental.pallas import tpu as pltpu
from jax.sharding import PartitionSpec as P

NPHI = 8192
ROWS_DEV = 32
TR, TC = 16, 128
MESH = pl.DeviceIdType.MESH
TAP_SCALE = -math.log2(math.e) / 8.0


def split(x):
    high = x.astype(jnp.bfloat16)
    return high, (x - high.astype(jnp.float32)).astype(jnp.bfloat16)


def cos_sin(quarters):
    whole = jnp.floor(quarters + 0.5)
    angle = (quarters - whole) * (math.pi / 2.0)
    square = angle * angle
    sine = angle * (1.0 + square * (-1.0 / 6 + square * (1.0 / 120 + square * (-1.0 / 5040))))
    cosine = 1.0 + square * (-0.5 + square * (1.0 / 24 + square * (-1.0 / 720 + square * (1.0 / 40320))))
    quadrant = whole.astype(jnp.int32)
    swapped = (quadrant & 1) != 0
    first = jnp.where(swapped, sine, cosine)
    second = jnp.where(swapped, cosine, sine)
    first = jnp.where(((quadrant + 1) & 2) != 0, -first, first)
    second = jnp.where((quadrant & 2) != 0, -second, second)
    return first, second


def nt_dot(a, b):
    return lax.dot_general(a, b, (((1,), (1,)), ((), ())), preferred_element_type=jnp.float32)


def spectra_kernel(bands, lons, subs, lag, unroll, target_hbm, qu_hbm, off_hbm, rb_hbm, cb_hbm, orders_hbm, out_ref,
                   target_ref, qu_ref, off_ref, rb_ref, cb_ref, orders_ref, keys_row, keys, sums, tiles, halo, order_col, t_hi, t_lo,
                   turn, spin, held, g_hi, g_lo, part, arrived, total, landed, ready, in_sem, keys_sem, halo_send, halo_recv, x_send, x_recv, a_send, a_recv):
    band = lax.axis_index("band")
    lon = lax.axis_index("lon")
    run = bands // subs
    per_sub = 2 * run
    per_group = per_sub * lons
    per_lon = 2 * bands
    quarter = band // run
    above = lax.rem(band + bands - 1, bands)
    below = lax.rem(band + 1, bands)
    blocks = rb_ref.shape[0]

    arrays = ((target_hbm, target_ref), (cb_hbm, cb_ref), (rb_hbm, rb_ref), (off_hbm, off_ref), (qu_hbm, qu_ref),
              (orders_hbm, orders_ref))
    inputs = [pltpu.make_async_copy(source, here, in_sem.at[i]) for i, (source, here) in enumerate(arrays)]
    for copy in inputs:
        copy.start()

    width = bands // 8
    first_of_row = band // width * width

    def in_row(step):
        return first_of_row + lax.rem(band + step, width)

    barrier = pltpu.get_barrier_semaphore()
    greeted = [(above, lon), (below, lon)]
    greeted += [(band, lax.rem(lon + step, lons)) for step in range(1, lons)]
    greeted += [(in_row(step), lon) for step in range(1, width)]
    greeted += [(lax.rem(band + step * width, bands), lon) for step in range(1, bands // width)]
    for place in greeted:
        pl.semaphore_signal(barrier, inc=1, device_id=place, device_id_type=MESH)

    inputs[0].wait()
    lane128 = lax.broadcasted_iota(jnp.int32, (1, 128), 1)
    row_keys, col_keys = [], []
    for h in range(blocks // 128):
        row = (target_ref[:, h * 128:h * 128 + 128] * blocks + (lane128 + h * 128)).astype(jnp.float32)
        row_keys.append(row)
        col_keys.append(jnp.transpose(jnp.broadcast_to(row, (128, 128))))
    ranks = []
    for col in col_keys:
        before = jnp.zeros((128, 128), jnp.float32)
        for row in row_keys:
            before = before + jnp.where(row < col, 1.0, 0.0)
        ranks.append(jnp.sum(before, 1, keepdims=True))
    through = jnp.zeros((1, 128), jnp.float32)
    ahead = jnp.zeros((1, 128), jnp.float32)
    first_key = (lane128 * blocks).astype(jnp.float32)
    for col in col_keys:
        ahead = ahead + jnp.sum(jnp.where(col < first_key, 1.0, 0.0), 0, keepdims=True)
        through = through + jnp.sum(jnp.where(col < first_key + blocks, 1.0, 0.0), 0, keepdims=True)
    last_place = jnp.where(through > ahead, through - 1.0, float(blocks))
    for h in range(blocks // 128):
        place = (lane128 + h * 128).astype(jnp.float32)
        row = jnp.zeros((1, 128), jnp.float32)
        for col, rank in zip(col_keys, ranks):
            row = row + jnp.sum(jnp.where(rank == place, col, 0.0), 0, keepdims=True)
        keys_row[pl.ds(h, 1), :] = row.astype(jnp.int32)
    keys_row[pl.ds(blocks // 128, 1), :] = last_place.astype(jnp.int32)
    sums[blocks] = jnp.zeros((2 * TR, TC), jnp.float32)
    to_scalars = pltpu.make_async_copy(keys_row, keys, keys_sem)
    to_scalars.start()
    to_scalars.wait()
    for copy in inputs[1:]:
        copy.wait()

    pos = lax.broadcasted_iota(jnp.int32, (TR, 128), 0)

    def block_tile(n):
        row = pl.ds(n, 1)
        cb = cb_ref[row, :]
        col_o = (pos - cb) & 15
        d = col_o.astype(jnp.float32) - (off_ref[1, row, :] + 3.0)
        v_hi, v_lo = split(jnp.exp2(d * d * TAP_SCALE))
        group = jnp.where(col_o < 8, cb + col_o - pos, -16).astype(jnp.bfloat16)
        zero = jnp.zeros((TR, 128), jnp.bfloat16)
        hi, lo = [], []
        for sixteen in range(TC // 16):
            here = group == jnp.bfloat16(16 * sixteen)
            hi.append(jnp.where(here, v_hi, zero))
            lo.append(jnp.where(here, v_lo, zero))
        cols = jnp.concatenate([jnp.concatenate(hi, 0), jnp.concatenate(lo, 0)], 1)
        row_o = (pos - rb_ref[row, :]) & 15
        e = row_o.astype(jnp.float32) - (off_ref[0, row, :] + 3.0)
        a = jnp.where(row_o < 8, jnp.exp2(e * e * TAP_SCALE), 0.0)
        q_hi, q_lo = split(a * qu_ref[0, row, :])
        u_hi, u_lo = split(a * qu_ref[1, row, :])
        half = jnp.concatenate([q_hi, u_hi, q_lo, u_lo], 0)
        out = jnp.transpose(nt_dot(cols, jnp.concatenate([half, half], 1)))
        return out[:2 * TR] + out[2 * TR:]

    key_bits = blocks.bit_length() - 1

    def deposit(i, carry):
        running, last_tile = carry
        for j in range(unroll):
            place = i * unroll + j
            key = keys[place // 128, place % 128]
            tile = key >> key_bits
            same = jnp.where(tile == last_tile, 1.0, 0.0)
            running = running * same + block_tile(key & (blocks - 1))
            sums[place] = running
            last_tile = tile
        return running, last_tile

    lax.fori_loop(0, blocks // unroll, deposit, (jnp.zeros((2 * TR, TC), jnp.float32), jnp.int32(-1)))

    def gather(tile, carry):
        tiles[tile] = sums[jnp.clip(keys[blocks // 128, tile], 0, blocks)]
        return carry

    lax.fori_loop(0, 16, gather, 0, unroll=16)
    lax.fori_loop(48, 64, gather, 0, unroll=16)
    pl.semaphore_wait(barrier, len(greeted))

    def to_band(toward, part_of):
        return pltpu.make_async_remote_copy(
            src_ref=tiles.at[pl.ds(48 * (1 - toward) + 8 * part_of, 8)], dst_ref=halo.at[toward, pl.ds(8 * part_of, 8)],
            send_sem=halo_send.at[toward, part_of], recv_sem=halo_recv.at[toward, part_of],
            device_id=(above if toward else below, lon), device_id_type=MESH)

    even = lax.rem(band, 2) == 0
    for part_of in (1, 0):
        @pl.when(even)
        def _():
            to_band(1, part_of).start()
            to_band(0, part_of).start()

        @pl.when(jnp.logical_not(even))
        def _():
            to_band(0, part_of).start()
            to_band(1, part_of).start()

    for step in range(1, width):
        pl.semaphore_signal(ready, inc=1, device_id=(in_row(step), lon), device_id_type=MESH)

    lax.fori_loop(16, 48, gather, 0, unroll=16)

    lane = lax.broadcasted_iota(jnp.int32, (1, 128), 1)
    half = lane // 64
    for row in range(8):
        order_col[pl.ds(row * 128, 128), :] = jnp.transpose(
            jnp.broadcast_to(orders_ref[pl.ds(row, 1), :].astype(jnp.float32), (128, 128)))
    cycle = band * ROWS_DEV + ((lane // 32) % 2) * TR + lane % 16
    _, sine = cos_sin((cycle.astype(jnp.float32) + 0.5) * (1.0 / 2048))
    weight = sine * (math.pi * math.sqrt(2.0 / (bands * ROWS_DEV * NPHI)))
    low_columns = lane.astype(jnp.float32) * (1.0 / 2048)
    spin_phase = (half * 256 + lon * 2048).astype(jnp.float32) * (1.0 / 2048)

    def table(step, carry):
        group = step // lons
        ell = lax.rem(step, lons)
        first = group * per_group + 2 * ell
        m = jnp.concatenate([order_col[pl.ds(first + place, run, stride=2 * lons), :] for place in range(2)], 0)
        rows = pl.ds(pl.multiple_of(ell * 2 * run, 2 * run), 2 * run)
        sine_rows = pl.ds(pl.multiple_of(per_group + ell * 2 * run, 2 * run), 2 * run)
        for side in range(2):
            c, s = cos_sin(m * (low_columns + side * (128.0 / 2048)))
            c_hi, c_lo = split(c)
            s_hi, s_lo = split(-s)
            cols = pl.ds(side * 128, 128)
            t_hi[group, rows, cols] = c_hi
            t_lo[group, rows, cols] = c_lo
            t_hi[group, sine_rows, cols] = s_hi
            t_lo[group, sine_rows, cols] = s_lo
        c, s = cos_sin(m * (512.0 / 2048))
        turn[group, 0, rows, :] = c
        turn[group, 1, rows, :] = -s
        least = (m.astype(jnp.int32) & 31).astype(jnp.float32)
        c, s = cos_sin(least * spin_phase)
        spin[group, 0, rows, :] = c * weight
        spin[group, 1, rows, :] = -s * weight
        return carry

    lax.fori_loop(0, subs * lons, table, 0)

    def columns_of(part_of):
        for toward in range(2):
            to_band(toward, part_of).wait_recv()
        for v in range(2 * part_of, 2 * part_of + 2):
            for k in range(2):
                pieces = []
                for h in range(2):
                    for tr in range(2):
                        tile = 2 * (2 * v + h) + k
                        pieces.append(tiles[16 * (tr + 1) + tile] + halo[tr, tile])
                hi, lo = split(jnp.transpose(jnp.concatenate(pieces, 0)))
                g_hi[pl.ds(k * 128, 128), pl.ds(v * 128, 128)] = hi
                g_lo[pl.ds(k * 128, 128), pl.ds(v * 128, 128)] = lo

    def product(group, part_of):
        cols = pl.ds(part_of * 256, 256)
        value = (jnp.dot(t_hi[group], g_hi[:, cols], preferred_element_type=jnp.float32)
                 + jnp.dot(t_hi[group], g_lo[:, cols], preferred_element_type=jnp.float32)
                 + jnp.dot(t_lo[group], g_hi[:, cols], preferred_element_type=jnp.float32))
        return value[:per_group], value[per_group:]

    columns_of(1)

    def begin(group, carry):
        c, s = product(group, 1)
        wr = turn[group, 0]
        wi = turn[group, 1]
        re, im = c[:, 128:], s[:, 128:]
        held[group, 0] = re * wr - im * wi + c[:, :128]
        held[group, 1] = re * wi + im * wr + s[:, :128]
        return carry

    lax.fori_loop(0, subs, begin, 0)
    columns_of(0)

    is_real = lane < 64

    def transform(group):
        c, s = product(group, 0)
        wr = turn[group, 0]
        wi = turn[group, 1]
        re, im = held[group, 0], held[group, 1]
        for side in (1, 0):
            c1 = c[:, side * 128:side * 128 + 128]
            s1 = s[:, side * 128:side * 128 + 128]
            re, im = re * wr - im * wi + c1, re * wi + im * wr + s1
        pr = spin[group, 0]
        pi = spin[group, 1]
        zr = re * pr - im * pi
        zi = re * pi + im * pr
        zr = zr + pltpu.roll(zr, 64, 1)
        zi = zi + pltpu.roll(zi, 64, 1)
        z = jnp.where(is_real, zr, zi)
        for k in range(per_group // run):
            ell, place = divmod(k, 2)
            part[group, ell, pl.ds(place, run, stride=2), :] = z[k * run:(k + 1) * run]

    def over_lon(step, group, sub):
        ell = lax.rem(lon + step, lons)
        return pltpu.make_async_remote_copy(
            src_ref=part.at[group, ell], dst_ref=arrived.at[group, lons - step],
            send_sem=x_send.at[step, sub], recv_sem=x_recv.at[lons - step, sub],
            device_id=(band, ell), device_id_type=MESH)

    def far(step):
        return -min(step // 2 % 8, 8 - step // 2 % 8)

    def group_of(sub):
        ahead = jnp.int32(0)
        for i, step in enumerate(sorted(range(1, subs), key=lambda step: -min(step, subs - step))):
            ahead = jnp.where(sub == i, step, ahead)
        return lax.rem(quarter + ahead, subs)

    def send_part(sub, carry):
        group = group_of(sub)
        transform(group)
        for step in (2, 1, 3):
            over_lon(step, group, sub).start()
        return carry

    def send_total(sub, carry):
        group = group_of(sub)
        value = part[group, lon]
        for step in range(1, lons):
            over_lon(step, group, sub).wait_recv()
            value = value + arrived[group, lons - step]
        rows = pl.ds(pl.multiple_of(group * per_sub, per_sub), per_sub)
        total[rows, :] = value

        def send_one(target):
            pltpu.make_async_remote_copy(
                src_ref=total.at[pl.ds(2 * target, 2), :], dst_ref=landed.at[pl.ds(2 * band, 2), :],
                send_sem=a_send, recv_sem=a_recv, device_id=(target, lon), device_id_type=MESH).start()

        for step in sorted(range(1, run), key=far):
            send_one(group * run + lax.rem(band + step, run))

        @pl.when(group != quarter)
        def _():
            send_one(group * run + lax.rem(band, run))
        return carry

    def pipeline(sub, carry):
        @pl.when(sub < subs)
        def _():
            send_part(sub, 0)

        @pl.when(sub == lag)
        def _():
            pl.semaphore_wait(ready, width - 1)

        @pl.when(sub >= lag)
        def _():
            send_total(sub - lag, 0)
        return carry

    lax.fori_loop(0, subs + lag, pipeline, 0)

    own = pltpu.make_async_copy(total.at[pl.ds(2 * band, 2), :], landed.at[pl.ds(2 * band, 2), :], a_recv)
    own.start()
    pltpu.make_async_copy(landed, landed, a_recv).wait()

    lanes = lax.broadcasted_iota(jnp.int32, (bands // 4, 128), 1)
    for i in range(2):
        for f in range(2):
            for reim in range(2):
                value = jnp.zeros((bands // 4, 128), jnp.float32)
                for q in range(4):
                    x = landed[pl.ds(2 * q + i, bands // 4, stride=8), :]
                    for tr in range(2):
                        source = reim * 4 + tr * 2 + f
                        target = 2 * q + tr
                        moved = x if source == target else pltpu.roll(x, ((target - source) % 8) * 16, 1)
                        value = jnp.where(lanes // 16 == target, moved, value)
                for j in range(bands // 4):
                    out_ref[i, pl.ds(2 * f + reim, 1), pl.ds(j * 128, 128)] = value[j:j + 1, :]

    for part_of in range(2):
        for toward in range(2):
            to_band(toward, part_of).wait_send()
    for sub in range(subs):
        for step in range(1, lons):
            over_lon(step, group_of(sub), sub).wait_send()
    others = pl.ds(0, per_lon - 2)
    pltpu.make_async_copy(total.at[others], total.at[others], a_send).wait()


def spectra(targets, qu, off, rb, cb, orders, bands, lons, subs=4, lag=3, unroll=64):
    V = pl.BlockSpec(memory_space=pltpu.VMEM)
    f32, bf16 = jnp.float32, jnp.bfloat16
    blocks = rb.shape[0]
    return pl.pallas_call(
        functools.partial(spectra_kernel, bands, lons, subs, lag, unroll),
        out_shape=jax.ShapeDtypeStruct((2, 4, bands * ROWS_DEV), f32),
        in_specs=[pl.BlockSpec(memory_space=pl.ANY)] * 6,
        out_specs=V,
        scratch_shapes=[
            pltpu.VMEM(targets.shape, jnp.int32),
            pltpu.VMEM(qu.shape, f32),
            pltpu.VMEM(off.shape, f32),
            pltpu.VMEM(rb.shape, jnp.int32),
            pltpu.VMEM(cb.shape, jnp.int32),
            pltpu.VMEM(orders.shape, jnp.int32),
            pltpu.VMEM((8, 128), jnp.int32),
            pltpu.SMEM((8, 128), jnp.int32),
            pltpu.VMEM((blocks + 1, 2 * TR, TC), f32),
            pltpu.VMEM((64, 2 * TR, TC), f32),
            pltpu.VMEM((2, 16, 2 * TR, TC), f32),
            pltpu.VMEM((1024, 128), f32),
            pltpu.VMEM((subs, 512, 256), bf16),
            pltpu.VMEM((subs, 512, 256), bf16),
            pltpu.VMEM((subs, 2, 256, 128), f32),
            pltpu.VMEM((subs, 2, 256, 128), f32),
            pltpu.VMEM((subs, 2, 256, 128), f32),
            pltpu.VMEM((256, 512), bf16),
            pltpu.VMEM((256, 512), bf16),
            pltpu.VMEM((subs, lons, 256 // subs, 128), f32),
            pltpu.VMEM((subs, lons, 256 // subs, 128), f32),
            pltpu.VMEM((256, 128), f32),
            pltpu.VMEM((256, 128), f32),
            pltpu.SemaphoreType.REGULAR,
            pltpu.SemaphoreType.DMA((6,)),
            pltpu.SemaphoreType.DMA,
            pltpu.SemaphoreType.DMA((2, 2)),
            pltpu.SemaphoreType.DMA((2, 2)),
            pltpu.SemaphoreType.DMA((lons, subs)),
            pltpu.SemaphoreType.DMA((lons, subs)),
            pltpu.SemaphoreType.DMA,
            pltpu.SemaphoreType.DMA,
        ],
        compiler_params=pltpu.CompilerParams(collective_id=0, has_side_effects=True, vmem_limit_bytes=63 * 1024 * 1024),
    )(targets, qu, off, rb, cb, orders)


def body(qu_values, tap_offsets, row_base, col_base, tile_of_block, m_orders):
    bands = lax.axis_size("band")
    lons = lax.axis_size("lon")
    return spectra(tile_of_block.reshape(1, -1), qu_values, tap_offsets, row_base, col_base, m_orders.reshape(8, 128),
                   bands, lons)


def solution(mesh):
    placed = (
        P(None, ("band", "lon"), None),
        P(None, ("band", "lon"), None),
        P(("band", "lon"), None),
        P(("band", "lon"), None),
        P(("band", "lon")),
        P(),
    )
    return jax.shard_map(
        body, mesh=mesh, in_specs=placed, out_specs=P(("band", "lon"), None, None), check_vma=False
    )
```

```python
import functools, math
import jax, jax.numpy as jnp
from jax import lax
from jax.experimental import pallas as pl
from jax.experimental.pallas import tpu as pltpu
from jax.sharding import PartitionSpec as P

NPHI = 8192
ROWS_DEV = 32
TR, TC = 16, 128
MESH = pl.DeviceIdType.MESH
TAP_SCALE = -math.log2(math.e) / 8.0


def split(x):
    high = x.astype(jnp.bfloat16)
    return high, (x - high.astype(jnp.float32)).astype(jnp.bfloat16)


def cos_sin(quarters):
    whole = jnp.floor(quarters + 0.5)
    angle = (quarters - whole) * (math.pi / 2.0)
    square = angle * angle
    sine = angle * (1.0 + square * (-1.0 / 6 + square * (1.0 / 120 + square * (-1.0 / 5040))))
    cosine = 1.0 + square * (-0.5 + square * (1.0 / 24 + square * (-1.0 / 720 + square * (1.0 / 40320))))
    quadrant = whole.astype(jnp.int32)
    swapped = (quadrant & 1) != 0
    first = jnp.where(swapped, sine, cosine)
    second = jnp.where(swapped, cosine, sine)
    first = jnp.where(((quadrant + 1) & 2) != 0, -first, first)
    second = jnp.where((quadrant & 2) != 0, -second, second)
    return first, second


def nt_dot(a, b):
    return lax.dot_general(a, b, (((1,), (1,)), ((), ())), preferred_element_type=jnp.float32)


def spectra_kernel(bands, lons, subs, lag, unroll, target_hbm, qu_hbm, off_hbm, rb_hbm, cb_hbm, orders_hbm, out_ref,
                   target_ref, qu_ref, off_ref, rb_ref, cb_ref, orders_ref, keys_row, keys, sums, tiles, halo, order_col, trig,
                   turn, spin, folded, part, arrived, total, landed, ready, in_sem, keys_sem, halo_send, halo_recv, x_send, x_recv, a_send, a_recv):
    band = lax.axis_index("band")
    lon = lax.axis_index("lon")
    run = bands // subs
    per_sub = 2 * run
    per_group = per_sub * lons
    per_lon = 2 * bands
    quarter = band // run
    above = lax.rem(band + bands - 1, bands)
    below = lax.rem(band + 1, bands)
    blocks = rb_ref.shape[0]

    arrays = ((target_hbm, target_ref), (cb_hbm, cb_ref), (rb_hbm, rb_ref), (off_hbm, off_ref), (qu_hbm, qu_ref),
              (orders_hbm, orders_ref))
    inputs = [pltpu.make_async_copy(source, here, in_sem.at[i]) for i, (source, here) in enumerate(arrays)]
    for copy in inputs:
        copy.start()

    width = bands // 8
    first_of_row = band // width * width

    def in_row(step):
        return first_of_row + lax.rem(band + step, width)

    barrier = pltpu.get_barrier_semaphore()
    greeted = [(above, lon), (below, lon)]
    greeted += [(band, lax.rem(lon + step, lons)) for step in range(1, lons)]
    greeted += [(in_row(step), lon) for step in range(1, width)]
    greeted += [(lax.rem(band + step * width, bands), lon) for step in range(1, bands // width)]
    for place in greeted:
        pl.semaphore_signal(barrier, inc=1, device_id=place, device_id_type=MESH)

    inputs[0].wait()
    lane128 = lax.broadcasted_iota(jnp.int32, (1, 128), 1)
    row_keys, col_keys = [], []
    for h in range(blocks // 128):
        row = (target_ref[:, h * 128:h * 128 + 128] * blocks + (lane128 + h * 128)).astype(jnp.float32)
        row_keys.append(row)
        col_keys.append(jnp.transpose(jnp.broadcast_to(row, (128, 128))))
    ranks = []
    for col in col_keys:
        before = jnp.zeros((128, 128), jnp.float32)
        for row in row_keys:
            before = before + jnp.where(row < col, 1.0, 0.0)
        ranks.append(jnp.sum(before, 1, keepdims=True))
    through = jnp.zeros((1, 128), jnp.float32)
    ahead = jnp.zeros((1, 128), jnp.float32)
    first_key = (lane128 * blocks).astype(jnp.float32)
    for col in col_keys:
        ahead = ahead + jnp.sum(jnp.where(col < first_key, 1.0, 0.0), 0, keepdims=True)
        through = through + jnp.sum(jnp.where(col < first_key + blocks, 1.0, 0.0), 0, keepdims=True)
    last_place = jnp.where(through > ahead, through - 1.0, float(blocks))
    for h in range(blocks // 128):
        place = (lane128 + h * 128).astype(jnp.float32)
        row = jnp.zeros((1, 128), jnp.float32)
        for col, rank in zip(col_keys, ranks):
            row = row + jnp.sum(jnp.where(rank == place, col, 0.0), 0, keepdims=True)
        keys_row[pl.ds(h, 1), :] = row.astype(jnp.int32)
    keys_row[pl.ds(blocks // 128, 1), :] = last_place.astype(jnp.int32)
    sums[blocks] = jnp.zeros((2 * TR, TC), jnp.float32)
    to_scalars = pltpu.make_async_copy(keys_row, keys, keys_sem)
    to_scalars.start()
    to_scalars.wait()
    for copy in inputs[1:]:
        copy.wait()

    pos = lax.broadcasted_iota(jnp.int32, (TR, 128), 0)

    def block_tile(n):
        row = pl.ds(n, 1)
        cb = cb_ref[row, :]
        col_o = (pos - cb) & 15
        d = col_o.astype(jnp.float32) - (off_ref[1, row, :] + 3.0)
        v_hi, v_lo = split(jnp.exp2(d * d * TAP_SCALE))
        group = jnp.where(col_o < 8, cb + col_o - pos, -16).astype(jnp.bfloat16)
        zero = jnp.zeros((TR, 128), jnp.bfloat16)
        hi, lo = [], []
        for sixteen in range(TC // 16):
            here = group == jnp.bfloat16(16 * sixteen)
            hi.append(jnp.where(here, v_hi, zero))
            lo.append(jnp.where(here, v_lo, zero))
        cols = jnp.concatenate([jnp.concatenate(hi, 0), jnp.concatenate(lo, 0)], 1)
        row_o = (pos - rb_ref[row, :]) & 15
        e = row_o.astype(jnp.float32) - (off_ref[0, row, :] + 3.0)
        a = jnp.where(row_o < 8, jnp.exp2(e * e * TAP_SCALE), 0.0)
        q_hi, q_lo = split(a * qu_ref[0, row, :])
        u_hi, u_lo = split(a * qu_ref[1, row, :])
        half = jnp.concatenate([q_hi, u_hi, q_lo, u_lo], 0)
        out = jnp.transpose(nt_dot(cols, jnp.concatenate([half, half], 1)))
        return out[:2 * TR] + out[2 * TR:]

    key_bits = blocks.bit_length() - 1

    def deposit(i, carry):
        running, last_tile = carry
        for j in range(unroll):
            place = i * unroll + j
            key = keys[place // 128, place % 128]
            tile = key >> key_bits
            same = jnp.where(tile == last_tile, 1.0, 0.0)
            running = running * same + block_tile(key & (blocks - 1))
            sums[place] = running
            last_tile = tile
        return running, last_tile

    lax.fori_loop(0, blocks // unroll, deposit, (jnp.zeros((2 * TR, TC), jnp.float32), jnp.int32(-1)))

    def gather(tile, carry):
        tiles[tile] = sums[jnp.clip(keys[blocks // 128, tile], 0, blocks)]
        return carry

    lax.fori_loop(0, 16, gather, 0, unroll=16)
    lax.fori_loop(48, 64, gather, 0, unroll=16)
    pl.semaphore_wait(barrier, len(greeted))

    upward = pltpu.make_async_remote_copy(
        src_ref=tiles.at[pl.ds(0, 16)], dst_ref=halo.at[1], send_sem=halo_send.at[0], recv_sem=halo_recv.at[1],
        device_id=(above, lon), device_id_type=MESH)
    downward = pltpu.make_async_remote_copy(
        src_ref=tiles.at[pl.ds(48, 16)], dst_ref=halo.at[0], send_sem=halo_send.at[1], recv_sem=halo_recv.at[0],
        device_id=(below, lon), device_id_type=MESH)
    upward.start()
    downward.start()
    for step in range(1, width):
        pl.semaphore_signal(ready, inc=1, device_id=(in_row(step), lon), device_id_type=MESH)

    lax.fori_loop(16, 48, gather, 0, unroll=16)

    lane = lax.broadcasted_iota(jnp.int32, (1, 128), 1)
    half = lane // 64
    for row in range(8):
        order_col[pl.ds(row * 128, 128), :] = jnp.transpose(
            jnp.broadcast_to(orders_ref[pl.ds(row, 1), :].astype(jnp.float32), (128, 128)))
    cycle = band * ROWS_DEV + ((lane // 32) % 2) * TR + lane % 16
    _, sine = cos_sin((cycle.astype(jnp.float32) + 0.5) * (1.0 / 2048))
    weight = sine * (math.pi * math.sqrt(2.0 / (bands * ROWS_DEV * NPHI)))
    half_columns = (lane.astype(jnp.float32) + 0.5) * (1.0 / 2048)
    spin_phase = (half * 1024 + lon * 2048).astype(jnp.float32) * (1.0 / 2048)

    def table(step, carry):
        group = step // lons
        ell = lax.rem(step, lons)
        first = group * per_group + 2 * ell
        m = jnp.concatenate([order_col[pl.ds(first + place, run, stride=2 * lons), :] for place in range(2)], 0)
        rows = pl.ds(pl.multiple_of(ell * 2 * run, 2 * run), 2 * run)
        low_rows = pl.ds(pl.multiple_of(per_group + ell * 2 * run, 2 * run), 2 * run)
        c, s = cos_sin(m * half_columns)
        for q, value in enumerate((c, -s)):
            hi, lo = split(value)
            trig[group, q, rows, :] = jnp.concatenate([hi, hi], 1)
            trig[group, q, low_rows, :] = jnp.concatenate([lo, lo], 1)
        c, s = cos_sin(m * (256.0 / 2048))
        turn[group, 0, rows, :] = c
        turn[group, 1, rows, :] = -s
        eighth = (m.astype(jnp.int32) & 7).astype(jnp.float32)
        c, s = cos_sin(eighth * spin_phase + m * (127.5 / 2048))
        spin[group, 0, rows, :] = c * weight
        spin[group, 1, rows, :] = -s * weight
        return carry

    lax.fori_loop(0, subs * lons, table, 0)

    upward.wait_recv()
    downward.wait_recv()

    sides = []
    for k in range(2):
        columns = []
        for v in range(4):
            pieces = []
            for h in range(2):
                for tr in range(2):
                    tile = 2 * (v + 4 * h) + k
                    pieces.append(tiles[16 * (tr + 1) + tile] + halo[tr, tile])
            columns.append(jnp.transpose(jnp.concatenate(pieces, 0)))
        sides.append(jnp.concatenate(columns, 1))
    flip = (lax.broadcasted_iota(jnp.int32, (128, 128), 0) + lax.broadcasted_iota(jnp.int32, (128, 128), 1)) == 127
    flip = jnp.where(flip, 1.0, 0.0).astype(jnp.bfloat16)
    hi, lo = split(sides[0])
    turned = (jnp.dot(flip, hi, preferred_element_type=jnp.float32)
              + jnp.dot(flip, lo, preferred_element_type=jnp.float32))
    for q, value in enumerate((sides[1] + turned, sides[1] - turned)):
        hi, lo = split(value)
        folded[q, pl.ds(0, 128), :] = hi
        folded[q, pl.ds(128, 128), :] = lo

    is_real = lane < 64

    def transform(group):
        def product(v, q):
            value = jnp.dot(trig[group, q], folded[q, :, pl.ds(v * 128, 256)], preferred_element_type=jnp.float32)
            return value[:per_group] + value[per_group:]

        wr = turn[group, 0]
        wi = turn[group, 1]
        re = im = None
        for v in (2, 0):
            c, s = product(v, 0), product(v, 1)
            for side in (1, 0):
                c1 = c[:, side * 128:side * 128 + 128]
                s1 = s[:, side * 128:side * 128 + 128]
                re, im = (c1, s1) if re is None else (re * wr - im * wi + c1, re * wi + im * wr + s1)
        pr = spin[group, 0]
        pi = spin[group, 1]
        zr = re * pr - im * pi
        zi = re * pi + im * pr
        zr = zr + pltpu.roll(zr, 64, 1)
        zi = zi + pltpu.roll(zi, 64, 1)
        z = jnp.where(is_real, zr, zi)
        for k in range(per_group // run):
            ell, place = divmod(k, 2)
            part[group, ell, pl.ds(place, run, stride=2), :] = z[k * run:(k + 1) * run]

    def over_lon(step, group, sub):
        ell = lax.rem(lon + step, lons)
        return pltpu.make_async_remote_copy(
            src_ref=part.at[group, ell], dst_ref=arrived.at[group, lons - step],
            send_sem=x_send.at[step, sub], recv_sem=x_recv.at[lons - step, sub],
            device_id=(band, ell), device_id_type=MESH)

    def far(step):
        return -min(step // 2 % 8, 8 - step // 2 % 8)

    def group_of(sub):
        ahead = jnp.int32(0)
        for i, step in enumerate(sorted(range(1, subs), key=lambda step: -min(step, subs - step))):
            ahead = jnp.where(sub == i, step, ahead)
        return lax.rem(quarter + ahead, subs)

    def send_part(sub, carry):
        group = group_of(sub)
        transform(group)
        for step in (2, 1, 3):
            over_lon(step, group, sub).start()
        return carry

    def send_total(sub, carry):
        group = group_of(sub)
        value = part[group, lon]
        for step in range(1, lons):
            over_lon(step, group, sub).wait_recv()
            value = value + arrived[group, lons - step]
        rows = pl.ds(pl.multiple_of(group * per_sub, per_sub), per_sub)
        total[rows, :] = value

        def send_one(target):
            pltpu.make_async_remote_copy(
                src_ref=total.at[pl.ds(2 * target, 2), :], dst_ref=landed.at[pl.ds(2 * band, 2), :],
                send_sem=a_send, recv_sem=a_recv, device_id=(target, lon), device_id_type=MESH).start()

        for step in sorted(range(1, run), key=far):
            send_one(group * run + lax.rem(band + step, run))

        @pl.when(group != quarter)
        def _():
            send_one(group * run + lax.rem(band, run))
        return carry

    def pipeline(sub, carry):
        @pl.when(sub < subs)
        def _():
            send_part(sub, 0)

        @pl.when(sub == lag)
        def _():
            pl.semaphore_wait(ready, width - 1)

        @pl.when(sub >= lag)
        def _():
            send_total(sub - lag, 0)
        return carry

    lax.fori_loop(0, subs + lag, pipeline, 0)

    own = pltpu.make_async_copy(total.at[pl.ds(2 * band, 2), :], landed.at[pl.ds(2 * band, 2), :], a_recv)
    own.start()
    pltpu.make_async_copy(landed, landed, a_recv).wait()

    lanes = lax.broadcasted_iota(jnp.int32, (bands // 4, 128), 1)
    for i in range(2):
        for f in range(2):
            for reim in range(2):
                value = jnp.zeros((bands // 4, 128), jnp.float32)
                for q in range(4):
                    x = landed[pl.ds(2 * q + i, bands // 4, stride=8), :]
                    for tr in range(2):
                        source = reim * 4 + tr * 2 + f
                        target = 2 * q + tr
                        moved = x if source == target else pltpu.roll(x, ((target - source) % 8) * 16, 1)
                        value = jnp.where(lanes // 16 == target, moved, value)
                for j in range(bands // 4):
                    out_ref[i, pl.ds(2 * f + reim, 1), pl.ds(j * 128, 128)] = value[j:j + 1, :]

    upward.wait_send()
    downward.wait_send()
    for sub in range(subs):
        for step in range(1, lons):
            over_lon(step, group_of(sub), sub).wait_send()
    others = pl.ds(0, per_lon - 2)
    pltpu.make_async_copy(total.at[others], total.at[others], a_send).wait()


def spectra(targets, qu, off, rb, cb, orders, bands, lons, subs=4, lag=3, unroll=64):
    V = pl.BlockSpec(memory_space=pltpu.VMEM)
    f32, bf16 = jnp.float32, jnp.bfloat16
    blocks = rb.shape[0]
    return pl.pallas_call(
        functools.partial(spectra_kernel, bands, lons, subs, lag, unroll),
        out_shape=jax.ShapeDtypeStruct((2, 4, bands * ROWS_DEV), f32),
        in_specs=[pl.BlockSpec(memory_space=pl.ANY)] * 6,
        out_specs=V,
        scratch_shapes=[
            pltpu.VMEM(targets.shape, jnp.int32),
            pltpu.VMEM(qu.shape, f32),
            pltpu.VMEM(off.shape, f32),
            pltpu.VMEM(rb.shape, jnp.int32),
            pltpu.VMEM(cb.shape, jnp.int32),
            pltpu.VMEM(orders.shape, jnp.int32),
            pltpu.VMEM((8, 128), jnp.int32),
            pltpu.SMEM((8, 128), jnp.int32),
            pltpu.VMEM((blocks + 1, 2 * TR, TC), f32),
            pltpu.VMEM((64, 2 * TR, TC), f32),
            pltpu.VMEM((2, 16, 2 * TR, TC), f32),
            pltpu.VMEM((1024, 128), f32),
            pltpu.VMEM((subs, 2, 512, 256), bf16),
            pltpu.VMEM((subs, 2, 256, 128), f32),
            pltpu.VMEM((subs, 2, 256, 128), f32),
            pltpu.VMEM((2, 256, 512), bf16),
            pltpu.VMEM((subs, lons, 256 // subs, 128), f32),
            pltpu.VMEM((subs, lons, 256 // subs, 128), f32),
            pltpu.VMEM((256, 128), f32),
            pltpu.VMEM((256, 128), f32),
            pltpu.SemaphoreType.REGULAR,
            pltpu.SemaphoreType.DMA((6,)),
            pltpu.SemaphoreType.DMA,
            pltpu.SemaphoreType.DMA((2,)),
            pltpu.SemaphoreType.DMA((2,)),
            pltpu.SemaphoreType.DMA((lons, subs)),
            pltpu.SemaphoreType.DMA((lons, subs)),
            pltpu.SemaphoreType.DMA,
            pltpu.SemaphoreType.DMA,
        ],
        compiler_params=pltpu.CompilerParams(collective_id=0, has_side_effects=True, vmem_limit_bytes=63 * 1024 * 1024),
    )(targets, qu, off, rb, cb, orders)


def body(qu_values, tap_offsets, row_base, col_base, tile_of_block, m_orders):
    bands = lax.axis_size("band")
    lons = lax.axis_size("lon")
    return spectra(tile_of_block.reshape(1, -1), qu_values, tap_offsets, row_base, col_base, m_orders.reshape(8, 128),
                   bands, lons)


def solution(mesh):
    placed = (
        P(None, ("band", "lon"), None),
        P(None, ("band", "lon"), None),
        P(("band", "lon"), None),
        P(("band", "lon"), None),
        P(("band", "lon")),
        P(),
    )
    return jax.shard_map(
        body, mesh=mesh, in_specs=placed, out_specs=P(("band", "lon"), None, None), check_vma=False
    )
```

```python
import functools, math
import jax, jax.numpy as jnp
from jax import lax
from jax.experimental import pallas as pl
from jax.experimental.pallas import tpu as pltpu
from jax.sharding import PartitionSpec as P

NPHI = 8192
ROWS_DEV = 32
TR, TC = 16, 128
MESH = pl.DeviceIdType.MESH
TAP_SCALE = -math.log2(math.e) / 8.0


def split(x):
    high = x.astype(jnp.bfloat16)
    return high, (x - high.astype(jnp.float32)).astype(jnp.bfloat16)


def cos_sin(quarters):
    whole = jnp.floor(quarters + 0.5)
    angle = (quarters - whole) * (math.pi / 2.0)
    square = angle * angle
    sine = angle * (1.0 + square * (-1.0 / 6 + square * (1.0 / 120 + square * (-1.0 / 5040))))
    cosine = 1.0 + square * (-0.5 + square * (1.0 / 24 + square * (-1.0 / 720 + square * (1.0 / 40320))))
    quadrant = whole.astype(jnp.int32)
    swapped = (quadrant & 1) != 0
    first = jnp.where(swapped, sine, cosine)
    second = jnp.where(swapped, cosine, sine)
    first = jnp.where(((quadrant + 1) & 2) != 0, -first, first)
    second = jnp.where((quadrant & 2) != 0, -second, second)
    return first, second


def nt_dot(a, b):
    return lax.dot_general(a, b, (((1,), (1,)), ((), ())), preferred_element_type=jnp.float32)


def spectra_kernel(bands, lons, subs, lag, unroll, target_hbm, qu_hbm, off_hbm, rb_hbm, cb_hbm, orders_hbm, out_ref,
                   target_ref, qu_ref, off_ref, rb_ref, cb_ref, orders_ref, keys_row, keys, sums, tiles, halo, order_col, trig,
                   turn, spin, folded, part, arrived, total, landed, ready, in_sem, keys_sem, halo_send, halo_recv, x_send, x_recv, a_send, a_recv):
    band = lax.axis_index("band")
    lon = lax.axis_index("lon")
    run = bands // subs
    per_sub = 2 * run
    per_group = per_sub * lons
    per_lon = 2 * bands
    quarter = band // run
    above = lax.rem(band + bands - 1, bands)
    below = lax.rem(band + 1, bands)
    blocks = rb_ref.shape[0]

    arrays = ((target_hbm, target_ref), (cb_hbm, cb_ref), (rb_hbm, rb_ref), (off_hbm, off_ref), (qu_hbm, qu_ref),
              (orders_hbm, orders_ref))
    inputs = [pltpu.make_async_copy(source, here, in_sem.at[i]) for i, (source, here) in enumerate(arrays)]
    for copy in inputs:
        copy.start()

    width = bands // 8
    first_of_row = band // width * width

    def in_row(step):
        return first_of_row + lax.rem(band + step, width)

    barrier = pltpu.get_barrier_semaphore()
    greeted = [(above, lon), (below, lon)]
    greeted += [(band, lax.rem(lon + step, lons)) for step in range(1, lons)]
    greeted += [(in_row(step), lon) for step in range(1, width)]
    greeted += [(lax.rem(band + step * width, bands), lon) for step in range(1, bands // width)]
    for place in greeted:
        pl.semaphore_signal(barrier, inc=1, device_id=place, device_id_type=MESH)

    inputs[0].wait()
    lane128 = lax.broadcasted_iota(jnp.int32, (1, 128), 1)
    row_keys, col_keys = [], []
    for h in range(blocks // 128):
        row = (target_ref[:, h * 128:h * 128 + 128] * blocks + (lane128 + h * 128)).astype(jnp.float32)
        row_keys.append(row)
        col_keys.append(jnp.transpose(jnp.broadcast_to(row, (128, 128))))
    ranks = []
    for col in col_keys:
        before = jnp.zeros((128, 128), jnp.float32)
        for row in row_keys:
            before = before + jnp.where(row < col, 1.0, 0.0)
        ranks.append(jnp.sum(before, 1, keepdims=True))
    through = jnp.zeros((1, 128), jnp.float32)
    ahead = jnp.zeros((1, 128), jnp.float32)
    first_key = (lane128 * blocks).astype(jnp.float32)
    for col in col_keys:
        ahead = ahead + jnp.sum(jnp.where(col < first_key, 1.0, 0.0), 0, keepdims=True)
        through = through + jnp.sum(jnp.where(col < first_key + blocks, 1.0, 0.0), 0, keepdims=True)
    last_place = jnp.where(through > ahead, through - 1.0, float(blocks))
    for h in range(blocks // 128):
        place = (lane128 + h * 128).astype(jnp.float32)
        row = jnp.zeros((1, 128), jnp.float32)
        for col, rank in zip(col_keys, ranks):
            row = row + jnp.sum(jnp.where(rank == place, col, 0.0), 0, keepdims=True)
        keys_row[pl.ds(h, 1), :] = row.astype(jnp.int32)
    keys_row[pl.ds(blocks // 128, 1), :] = last_place.astype(jnp.int32)
    sums[blocks] = jnp.zeros((2 * TR, TC), jnp.float32)
    to_scalars = pltpu.make_async_copy(keys_row, keys, keys_sem)
    to_scalars.start()
    to_scalars.wait()
    for copy in inputs[1:]:
        copy.wait()

    pos = lax.broadcasted_iota(jnp.int32, (TR, 128), 0)

    def block_tile(n):
        row = pl.ds(n, 1)
        cb = cb_ref[row, :]
        col_o = (pos - cb) & 15
        d = col_o.astype(jnp.float32) - (off_ref[1, row, :] + 3.0)
        v_hi, v_lo = split(jnp.exp2(d * d * TAP_SCALE))
        group = jnp.where(col_o < 8, cb + col_o - pos, -16).astype(jnp.bfloat16)
        zero = jnp.zeros((TR, 128), jnp.bfloat16)
        hi, lo = [], []
        for sixteen in range(TC // 16):
            here = group == jnp.bfloat16(16 * sixteen)
            hi.append(jnp.where(here, v_hi, zero))
            lo.append(jnp.where(here, v_lo, zero))
        cols = jnp.concatenate([jnp.concatenate(hi, 0), jnp.concatenate(lo, 0)], 1)
        row_o = (pos - rb_ref[row, :]) & 15
        e = row_o.astype(jnp.float32) - (off_ref[0, row, :] + 3.0)
        a = jnp.where(row_o < 8, jnp.exp2(e * e * TAP_SCALE), 0.0)
        q_hi, q_lo = split(a * qu_ref[0, row, :])
        u_hi, u_lo = split(a * qu_ref[1, row, :])
        half = jnp.concatenate([q_hi, u_hi, q_lo, u_lo], 0)
        out = jnp.transpose(nt_dot(cols, jnp.concatenate([half, half], 1)))
        return out[:2 * TR] + out[2 * TR:]

    key_bits = blocks.bit_length() - 1

    def deposit(i, carry):
        running, last_tile = carry
        for j in range(unroll):
            place = i * unroll + j
            key = keys[place // 128, place % 128]
            tile = key >> key_bits
            same = jnp.where(tile == last_tile, 1.0, 0.0)
            running = running * same + block_tile(key & (blocks - 1))
            sums[place] = running
            last_tile = tile
        return running, last_tile

    lax.fori_loop(0, blocks // unroll, deposit, (jnp.zeros((2 * TR, TC), jnp.float32), jnp.int32(-1)))

    def gather(tile, carry):
        tiles[tile] = sums[jnp.clip(keys[blocks // 128, tile], 0, blocks)]
        return carry

    lax.fori_loop(0, 16, gather, 0, unroll=16)
    lax.fori_loop(48, 64, gather, 0, unroll=16)
    pl.semaphore_wait(barrier, len(greeted))

    upward = pltpu.make_async_remote_copy(
        src_ref=tiles.at[pl.ds(0, 16)], dst_ref=halo.at[1], send_sem=halo_send.at[0], recv_sem=halo_recv.at[1],
        device_id=(above, lon), device_id_type=MESH)
    downward = pltpu.make_async_remote_copy(
        src_ref=tiles.at[pl.ds(48, 16)], dst_ref=halo.at[0], send_sem=halo_send.at[1], recv_sem=halo_recv.at[0],
        device_id=(below, lon), device_id_type=MESH)
    upward.start()
    downward.start()
    for step in range(1, width):
        pl.semaphore_signal(ready, inc=1, device_id=(in_row(step), lon), device_id_type=MESH)

    lax.fori_loop(16, 48, gather, 0, unroll=16)

    lane = lax.broadcasted_iota(jnp.int32, (1, 128), 1)
    half = lane // 64
    for row in range(8):
        order_col[pl.ds(row * 128, 128), :] = jnp.transpose(
            jnp.broadcast_to(orders_ref[pl.ds(row, 1), :].astype(jnp.float32), (128, 128)))
    cycle = band * ROWS_DEV + ((lane // 32) % 2) * TR + lane % 16
    _, sine = cos_sin((cycle.astype(jnp.float32) + 0.5) * (1.0 / 2048))
    weight = sine * (math.pi * math.sqrt(2.0 / (bands * ROWS_DEV * NPHI)))
    half_columns = (lane.astype(jnp.float32) + 0.5) * (1.0 / 2048)
    spin_phase = (half * 1024 + lon * 2048).astype(jnp.float32) * (1.0 / 2048)

    def table(step, carry):
        group = step // lons
        ell = lax.rem(step, lons)
        first = group * per_group + 2 * ell
        m = jnp.concatenate([order_col[pl.ds(first + place, run, stride=2 * lons), :] for place in range(2)], 0)
        rows = pl.ds(pl.multiple_of(ell * 2 * run, 2 * run), 2 * run)
        low_rows = pl.ds(pl.multiple_of(per_group + ell * 2 * run, 2 * run), 2 * run)
        c, s = cos_sin(m * half_columns)
        for q, value in enumerate((c, -s)):
            hi, lo = split(value)
            trig[group, q, rows, :] = jnp.concatenate([hi, hi], 1)
            trig[group, q, low_rows, :] = jnp.concatenate([lo, lo], 1)
        c, s = cos_sin(m * (256.0 / 2048))
        turn[group, 0, rows, :] = c
        turn[group, 1, rows, :] = -s
        eighth = (m.astype(jnp.int32) & 7).astype(jnp.float32)
        c, s = cos_sin(eighth * spin_phase + m * (127.5 / 2048))
        spin[group, 0, rows, :] = c * weight
        spin[group, 1, rows, :] = -s * weight
        return carry

    lax.fori_loop(0, subs * lons, table, 0)

    upward.wait_recv()
    downward.wait_recv()

    sides = []
    for k in range(2):
        columns = []
        for v in range(4):
            pieces = []
            for h in range(2):
                for tr in range(2):
                    tile = 2 * (v + 4 * h) + k
                    pieces.append(tiles[16 * (tr + 1) + tile] + halo[tr, tile])
            columns.append(jnp.transpose(jnp.concatenate(pieces, 0)))
        sides.append(jnp.concatenate(columns, 1))
    flip = (lax.broadcasted_iota(jnp.int32, (128, 128), 0) + lax.broadcasted_iota(jnp.int32, (128, 128), 1)) == 127
    flip = jnp.where(flip, 1.0, 0.0).astype(jnp.bfloat16)
    hi, lo = split(sides[0])
    turned = (jnp.dot(flip, hi, preferred_element_type=jnp.float32)
              + jnp.dot(flip, lo, preferred_element_type=jnp.float32))
    for q, value in enumerate((sides[1] + turned, sides[1] - turned)):
        hi, lo = split(value)
        folded[q, pl.ds(0, 128), :] = hi
        folded[q, pl.ds(128, 128), :] = lo

    is_real = lane < 64

    def transform(group):
        def product(v, q):
            value = jnp.dot(trig[group, q], folded[q, :, pl.ds(v * 128, 256)], preferred_element_type=jnp.float32)
            return value[:per_group] + value[per_group:]

        wr = turn[group, 0]
        wi = turn[group, 1]
        re = im = None
        for v in (2, 0):
            c, s = product(v, 0), product(v, 1)
            for side in (1, 0):
                c1 = c[:, side * 128:side * 128 + 128]
                s1 = s[:, side * 128:side * 128 + 128]
                re, im = (c1, s1) if re is None else (re * wr - im * wi + c1, re * wi + im * wr + s1)
        pr = spin[group, 0]
        pi = spin[group, 1]
        zr = re * pr - im * pi
        zi = re * pi + im * pr
        zr = zr + pltpu.roll(zr, 64, 1)
        zi = zi + pltpu.roll(zi, 64, 1)
        z = jnp.where(is_real, zr, zi)
        for k in range(per_group // run):
            ell, place = divmod(k, 2)
            part[group, ell, pl.ds(place, run, stride=2), :] = z[k * run:(k + 1) * run]

    def over_lon(step, group, sub):
        ell = lax.rem(lon + step, lons)
        return pltpu.make_async_remote_copy(
            src_ref=part.at[group, ell], dst_ref=arrived.at[group, lons - step],
            send_sem=x_send.at[step, sub], recv_sem=x_recv.at[lons - step, sub],
            device_id=(band, ell), device_id_type=MESH)

    def far(step):
        return -min(step // 2 % 8, 8 - step // 2 % 8)

    def group_of(sub):
        ahead = jnp.int32(0)
        for i, step in enumerate(sorted(range(1, subs), key=lambda step: -min(step, subs - step))):
            ahead = jnp.where(sub == i, step, ahead)
        return lax.rem(quarter + ahead, subs)

    def send_part(sub, carry):
        group = group_of(sub)
        transform(group)
        for step in (2, 1, 3):
            over_lon(step, group, sub).start()
        return carry

    def send_total(sub, carry):
        group = group_of(sub)
        value = part[group, lon]
        for step in range(1, lons):
            over_lon(step, group, sub).wait_recv()
            value = value + arrived[group, lons - step]
        rows = pl.ds(pl.multiple_of(group * per_sub, per_sub), per_sub)
        total[rows, :] = value

        def send_one(target):
            pltpu.make_async_remote_copy(
                src_ref=total.at[pl.ds(2 * target, 2), :], dst_ref=landed.at[pl.ds(2 * band, 2), :],
                send_sem=a_send, recv_sem=a_recv, device_id=(target, lon), device_id_type=MESH).start()

        for step in sorted(range(1, run), key=far):
            send_one(group * run + lax.rem(band + step, run))

        @pl.when(group != quarter)
        def _():
            send_one(group * run + lax.rem(band, run))
        return carry

    def pipeline(sub, carry):
        @pl.when(sub < subs)
        def _():
            send_part(sub, 0)

        @pl.when(sub == lag)
        def _():
            pl.semaphore_wait(ready, width - 1)

        @pl.when(sub >= lag)
        def _():
            send_total(sub - lag, 0)
        return carry

    lax.fori_loop(0, subs + lag, pipeline, 0)

    own = pltpu.make_async_copy(total.at[pl.ds(2 * band, 2), :], landed.at[pl.ds(2 * band, 2), :], a_recv)
    own.start()
    pltpu.make_async_copy(landed, landed, a_recv).wait()

    lanes = lax.broadcasted_iota(jnp.int32, (bands // 4, 128), 1)
    for i in range(2):
        for f in range(2):
            for reim in range(2):
                value = jnp.zeros((bands // 4, 128), jnp.float32)
                for q in range(4):
                    x = landed[pl.ds(2 * q + i, bands // 4, stride=8), :]
                    for tr in range(2):
                        source = reim * 4 + tr * 2 + f
                        target = 2 * q + tr
                        moved = x if source == target else pltpu.roll(x, ((target - source) % 8) * 16, 1)
                        value = jnp.where(lanes // 16 == target, moved, value)
                for j in range(bands // 4):
                    out_ref[i, pl.ds(2 * f + reim, 1), pl.ds(j * 128, 128)] = value[j:j + 1, :]

    upward.wait_send()
    downward.wait_send()
    for sub in range(subs):
        for step in range(1, lons):
            over_lon(step, group_of(sub), sub).wait_send()
    others = pl.ds(0, per_lon - 2)
    pltpu.make_async_copy(total.at[others], total.at[others], a_send).wait()


def spectra(targets, qu, off, rb, cb, orders, bands, lons, subs=4, lag=3, unroll=128):
    V = pl.BlockSpec(memory_space=pltpu.VMEM)
    f32, bf16 = jnp.float32, jnp.bfloat16
    blocks = rb.shape[0]
    return pl.pallas_call(
        functools.partial(spectra_kernel, bands, lons, subs, lag, unroll),
        out_shape=jax.ShapeDtypeStruct((2, 4, bands * ROWS_DEV), f32),
        in_specs=[pl.BlockSpec(memory_space=pl.ANY)] * 6,
        out_specs=V,
        scratch_shapes=[
            pltpu.VMEM(targets.shape, jnp.int32),
            pltpu.VMEM(qu.shape, f32),
            pltpu.VMEM(off.shape, f32),
            pltpu.VMEM(rb.shape, jnp.int32),
            pltpu.VMEM(cb.shape, jnp.int32),
            pltpu.VMEM(orders.shape, jnp.int32),
            pltpu.VMEM((8, 128), jnp.int32),
            pltpu.SMEM((8, 128), jnp.int32),
            pltpu.VMEM((blocks + 1, 2 * TR, TC), f32),
            pltpu.VMEM((64, 2 * TR, TC), f32),
            pltpu.VMEM((2, 16, 2 * TR, TC), f32),
            pltpu.VMEM((1024, 128), f32),
            pltpu.VMEM((subs, 2, 512, 256), bf16),
            pltpu.VMEM((subs, 2, 256, 128), f32),
            pltpu.VMEM((subs, 2, 256, 128), f32),
            pltpu.VMEM((2, 256, 512), bf16),
            pltpu.VMEM((subs, lons, 256 // subs, 128), f32),
            pltpu.VMEM((subs, lons, 256 // subs, 128), f32),
            pltpu.VMEM((256, 128), f32),
            pltpu.VMEM((256, 128), f32),
            pltpu.SemaphoreType.REGULAR,
            pltpu.SemaphoreType.DMA((6,)),
            pltpu.SemaphoreType.DMA,
            pltpu.SemaphoreType.DMA((2,)),
            pltpu.SemaphoreType.DMA((2,)),
            pltpu.SemaphoreType.DMA((lons, subs)),
            pltpu.SemaphoreType.DMA((lons, subs)),
            pltpu.SemaphoreType.DMA,
            pltpu.SemaphoreType.DMA,
        ],
        compiler_params=pltpu.CompilerParams(collective_id=0, has_side_effects=True, vmem_limit_bytes=63 * 1024 * 1024),
    )(targets, qu, off, rb, cb, orders)


def body(qu_values, tap_offsets, row_base, col_base, tile_of_block, m_orders):
    bands = lax.axis_size("band")
    lons = lax.axis_size("lon")
    return spectra(tile_of_block.reshape(1, -1), qu_values, tap_offsets, row_base, col_base, m_orders.reshape(8, 128),
                   bands, lons)


def solution(mesh):
    placed = (
        P(None, ("band", "lon"), None),
        P(None, ("band", "lon"), None),
        P(("band", "lon"), None),
        P(("band", "lon"), None),
        P(("band", "lon")),
        P(),
    )
    return jax.shard_map(
        body, mesh=mesh, in_specs=placed, out_specs=P(("band", "lon"), None, None), check_vma=False
    )
```

```python
import functools, math
import jax, jax.numpy as jnp
from jax import lax
from jax.experimental import pallas as pl
from jax.experimental.pallas import tpu as pltpu
from jax.sharding import PartitionSpec as P

NPHI = 8192
ROWS_DEV = 32
TR, TC = 16, 128
MESH = pl.DeviceIdType.MESH
TAP_SCALE = -math.log2(math.e) / 8.0


def split(x):
    high = x.astype(jnp.bfloat16)
    return high, (x - high.astype(jnp.float32)).astype(jnp.bfloat16)


def cos_sin(quarters):
    whole = jnp.floor(quarters + 0.5)
    angle = (quarters - whole) * (math.pi / 2.0)
    square = angle * angle
    sine = angle * (1.0 + square * (-1.0 / 6 + square * (1.0 / 120 + square * (-1.0 / 5040))))
    cosine = 1.0 + square * (-0.5 + square * (1.0 / 24 + square * (-1.0 / 720 + square * (1.0 / 40320))))
    quadrant = whole.astype(jnp.int32)
    swapped = (quadrant & 1) != 0
    first = jnp.where(swapped, sine, cosine)
    second = jnp.where(swapped, cosine, sine)
    first = jnp.where(((quadrant + 1) & 2) != 0, -first, first)
    second = jnp.where((quadrant & 2) != 0, -second, second)
    return first, second


def nt_dot(a, b):
    return lax.dot_general(a, b, (((1,), (1,)), ((), ())), preferred_element_type=jnp.float32)


def spectra_kernel(bands, lons, subs, lag, unroll, target_hbm, qu_hbm, off_hbm, rb_hbm, cb_hbm, orders_hbm, out_ref,
                   target_ref, qu_ref, off_ref, rb_ref, cb_ref, orders_ref, keys_row, keys, sums, tiles, halo, order_col, trig,
                   turn, spin, folded, part, arrived, total, landed, ready, in_sem, keys_sem, halo_send, halo_recv, x_send, x_recv, a_send, a_recv):
    band = lax.axis_index("band")
    lon = lax.axis_index("lon")
    run = bands // subs
    per_sub = 2 * run
    per_group = per_sub * lons
    per_lon = 2 * bands
    quarter = band // run
    above = lax.rem(band + bands - 1, bands)
    below = lax.rem(band + 1, bands)
    blocks = rb_ref.shape[0]

    arrays = ((target_hbm, target_ref), (cb_hbm, cb_ref), (rb_hbm, rb_ref), (off_hbm, off_ref), (qu_hbm, qu_ref),
              (orders_hbm, orders_ref))
    inputs = [pltpu.make_async_copy(source, here, in_sem.at[i]) for i, (source, here) in enumerate(arrays)]
    for copy in inputs:
        copy.start()

    width = bands // 8
    first_of_row = band // width * width

    def in_row(step):
        return first_of_row + lax.rem(band + step, width)

    barrier = pltpu.get_barrier_semaphore()
    greeted = [(above, lon), (below, lon)]
    greeted += [(band, lax.rem(lon + step, lons)) for step in range(1, lons)]
    greeted += [(in_row(step), lon) for step in range(1, width)]
    greeted += [(lax.rem(band + step * width, bands), lon) for step in range(1, bands // width)]
    for place in greeted:
        pl.semaphore_signal(barrier, inc=1, device_id=place, device_id_type=MESH)

    inputs[0].wait()
    lane128 = lax.broadcasted_iota(jnp.int32, (1, 128), 1)
    row_keys, col_keys = [], []
    for h in range(blocks // 128):
        row = (target_ref[:, h * 128:h * 128 + 128] * blocks + (lane128 + h * 128)).astype(jnp.float32)
        row_keys.append(row)
        col_keys.append(jnp.transpose(jnp.broadcast_to(row, (128, 128))))
    ranks = []
    for col in col_keys:
        before = jnp.zeros((128, 128), jnp.float32)
        for row in row_keys:
            before = before + jnp.where(row < col, 1.0, 0.0)
        ranks.append(jnp.sum(before, 1, keepdims=True))
    through = jnp.zeros((1, 128), jnp.float32)
    ahead = jnp.zeros((1, 128), jnp.float32)
    first_key = (lane128 * blocks).astype(jnp.float32)
    for col in col_keys:
        ahead = ahead + jnp.sum(jnp.where(col < first_key, 1.0, 0.0), 0, keepdims=True)
        through = through + jnp.sum(jnp.where(col < first_key + blocks, 1.0, 0.0), 0, keepdims=True)
    last_place = jnp.where(through > ahead, through - 1.0, float(blocks))
    for h in range(blocks // 128):
        place = (lane128 + h * 128).astype(jnp.float32)
        row = jnp.zeros((1, 128), jnp.float32)
        for col, rank in zip(col_keys, ranks):
            row = row + jnp.sum(jnp.where(rank == place, col, 0.0), 0, keepdims=True)
        keys_row[pl.ds(h, 1), :] = row.astype(jnp.int32)
    keys_row[pl.ds(blocks // 128, 1), :] = last_place.astype(jnp.int32)
    sums[blocks] = jnp.zeros((2 * TR, TC), jnp.float32)
    to_scalars = pltpu.make_async_copy(keys_row, keys, keys_sem)
    to_scalars.start()
    to_scalars.wait()
    for copy in inputs[1:]:
        copy.wait()

    pos = lax.broadcasted_iota(jnp.int32, (TR, 128), 0)

    def block_tile(n):
        row = pl.ds(n, 1)
        cb = cb_ref[row, :]
        col_o = (pos - cb) & 15
        d = col_o.astype(jnp.float32) - (off_ref[1, row, :] + 3.0)
        v_hi, v_lo = split(jnp.exp2(d * d * TAP_SCALE))
        group = jnp.where(col_o < 8, cb + col_o - pos, -16).astype(jnp.bfloat16)
        zero = jnp.zeros((TR, 128), jnp.bfloat16)
        hi, lo = [], []
        for sixteen in range(TC // 16):
            here = group == jnp.bfloat16(16 * sixteen)
            hi.append(jnp.where(here, v_hi, zero))
            lo.append(jnp.where(here, v_lo, zero))
        cols = jnp.concatenate([jnp.concatenate(hi, 0), jnp.concatenate(lo, 0)], 1)
        row_o = (pos - rb_ref[row, :]) & 15
        e = row_o.astype(jnp.float32) - (off_ref[0, row, :] + 3.0)
        a = jnp.where(row_o < 8, jnp.exp2(e * e * TAP_SCALE), 0.0)
        q_hi, q_lo = split(a * qu_ref[0, row, :])
        u_hi, u_lo = split(a * qu_ref[1, row, :])
        half = jnp.concatenate([q_hi, u_hi, q_lo, u_lo], 0)
        out = jnp.transpose(nt_dot(cols, jnp.concatenate([half, half], 1)))
        return out[:2 * TR] + out[2 * TR:]

    key_bits = blocks.bit_length() - 1

    def deposit(i, carry):
        running, last_tile = carry
        for j in range(unroll):
            place = i * unroll + j
            key = keys[place // 128, place % 128]
            tile = key >> key_bits
            same = jnp.where(tile == last_tile, 1.0, 0.0)
            running = running * same + block_tile(key & (blocks - 1))
            sums[place] = running
            last_tile = tile
        return running, last_tile

    lax.fori_loop(0, blocks // unroll, deposit, (jnp.zeros((2 * TR, TC), jnp.float32), jnp.int32(-1)))

    def gather(tile, carry):
        tiles[tile] = sums[jnp.clip(keys[blocks // 128, tile], 0, blocks)]
        return carry

    lax.fori_loop(0, 16, gather, 0, unroll=16)
    lax.fori_loop(48, 64, gather, 0, unroll=16)
    pl.semaphore_wait(barrier, len(greeted))

    upward = pltpu.make_async_remote_copy(
        src_ref=tiles.at[pl.ds(0, 16)], dst_ref=halo.at[1], send_sem=halo_send.at[0], recv_sem=halo_recv.at[1],
        device_id=(above, lon), device_id_type=MESH)
    downward = pltpu.make_async_remote_copy(
        src_ref=tiles.at[pl.ds(48, 16)], dst_ref=halo.at[0], send_sem=halo_send.at[1], recv_sem=halo_recv.at[0],
        device_id=(below, lon), device_id_type=MESH)
    upward.start()
    downward.start()
    for step in range(1, width):
        pl.semaphore_signal(ready, inc=1, device_id=(in_row(step), lon), device_id_type=MESH)

    lax.fori_loop(16, 48, gather, 0, unroll=16)

    lane = lax.broadcasted_iota(jnp.int32, (1, 128), 1)
    half = lane // 64
    for row in range(8):
        order_col[pl.ds(row * 128, 128), :] = jnp.transpose(
            jnp.broadcast_to(orders_ref[pl.ds(row, 1), :].astype(jnp.float32), (128, 128)))
    cycle = band * ROWS_DEV + ((lane // 32) % 2) * TR + lane % 16
    _, sine = cos_sin((cycle.astype(jnp.float32) + 0.5) * (1.0 / 2048))
    weight = sine * (math.pi * math.sqrt(2.0 / (bands * ROWS_DEV * NPHI)))
    half_columns = (lane.astype(jnp.float32) + 0.5) * (1.0 / 2048)
    spin_phase = (half * 1024 + lon * 2048).astype(jnp.float32) * (1.0 / 2048)

    def table(step, carry):
        group = step // lons
        ell = lax.rem(step, lons)
        first = group * per_group + 2 * ell
        m = jnp.concatenate([order_col[pl.ds(first + place, run, stride=2 * lons), :] for place in range(2)], 0)
        rows = pl.ds(pl.multiple_of(ell * 2 * run, 2 * run), 2 * run)
        low_rows = pl.ds(pl.multiple_of(per_group + ell * 2 * run, 2 * run), 2 * run)
        c, s = cos_sin(m * half_columns)
        for q, value in enumerate((c, -s)):
            hi, lo = split(value)
            trig[group, q, rows, :] = jnp.concatenate([hi, hi], 1)
            trig[group, q, low_rows, :] = jnp.concatenate([lo, lo], 1)
        c, s = cos_sin(m * (256.0 / 2048))
        turn[group, 0, rows, :] = c
        turn[group, 1, rows, :] = -s
        eighth = (m.astype(jnp.int32) & 7).astype(jnp.float32)
        c, s = cos_sin(eighth * spin_phase + m * (127.5 / 2048))
        spin[group, 0, rows, :] = c * weight
        spin[group, 1, rows, :] = -s * weight
        return carry

    lax.fori_loop(0, subs * lons, table, 0)

    upward.wait_recv()
    downward.wait_recv()

    sides = []
    for k in range(2):
        columns = []
        for v in range(4):
            pieces = []
            for h in range(2):
                for tr in range(2):
                    tile = 2 * (v + 4 * h) + k
                    pieces.append(tiles[16 * (tr + 1) + tile] + halo[tr, tile])
            columns.append(jnp.transpose(jnp.concatenate(pieces, 0)))
        sides.append(jnp.concatenate(columns, 1))
    flip = (lax.broadcasted_iota(jnp.int32, (128, 128), 0) + lax.broadcasted_iota(jnp.int32, (128, 128), 1)) == 127
    flip = jnp.where(flip, 1.0, 0.0).astype(jnp.bfloat16)
    hi, lo = split(sides[0])
    turned = (jnp.dot(flip, hi, preferred_element_type=jnp.float32)
              + jnp.dot(flip, lo, preferred_element_type=jnp.float32))
    for q, value in enumerate((sides[1] + turned, sides[1] - turned)):
        hi, lo = split(value)
        folded[q, pl.ds(0, 128), :] = hi
        folded[q, pl.ds(128, 128), :] = lo

    is_real = lane < 64

    def transform(group):
        def product(v, q):
            value = jnp.dot(trig[group, q], folded[q, :, pl.ds(v * 128, 256)], preferred_element_type=jnp.float32)
            return value[:per_group] + value[per_group:]

        wr = turn[group, 0]
        wi = turn[group, 1]
        re = im = None
        for v in (2, 0):
            c, s = product(v, 0), product(v, 1)
            for side in (1, 0):
                c1 = c[:, side * 128:side * 128 + 128]
                s1 = s[:, side * 128:side * 128 + 128]
                re, im = (c1, s1) if re is None else (re * wr - im * wi + c1, re * wi + im * wr + s1)
        pr = spin[group, 0]
        pi = spin[group, 1]
        zr = re * pr - im * pi
        zi = re * pi + im * pr
        zr = zr + pltpu.roll(zr, 64, 1)
        zi = zi + pltpu.roll(zi, 64, 1)
        z = jnp.where(is_real, zr, zi)
        for k in range(per_group // run):
            ell, place = divmod(k, 2)
            part[group, ell, pl.ds(place, run, stride=2), :] = z[k * run:(k + 1) * run]

    def over_lon(step, group, sub):
        ell = lax.rem(lon + step, lons)
        return pltpu.make_async_remote_copy(
            src_ref=part.at[group, ell], dst_ref=arrived.at[group, lons - step],
            send_sem=x_send.at[step, sub], recv_sem=x_recv.at[lons - step, sub],
            device_id=(band, ell), device_id_type=MESH)

    def far(step):
        return -min(step // 2 % 8, 8 - step // 2 % 8)

    def group_of(sub):
        ahead = jnp.int32(0)
        for i, step in enumerate(sorted(range(1, subs), key=lambda step: -min(step, subs - step))):
            ahead = jnp.where(sub == i, step, ahead)
        return lax.rem(quarter + ahead, subs)

    def send_part(sub, carry):
        group = group_of(sub)
        transform(group)
        for step in (2, 1, 3):
            over_lon(step, group, sub).start()
        return carry

    def send_total(sub, carry):
        group = group_of(sub)
        value = part[group, lon]
        for step in range(1, lons):
            over_lon(step, group, sub).wait_recv()
            value = value + arrived[group, lons - step]
        rows = pl.ds(pl.multiple_of(group * per_sub, per_sub), per_sub)
        total[rows, :] = value

        def send_one(target):
            pltpu.make_async_remote_copy(
                src_ref=total.at[pl.ds(2 * target, 2), :], dst_ref=landed.at[pl.ds(2 * band, 2), :],
                send_sem=a_send, recv_sem=a_recv, device_id=(target, lon), device_id_type=MESH).start()

        for step in sorted(range(1, run), key=far):
            send_one(group * run + lax.rem(band + step, run))

        @pl.when(group != quarter)
        def _():
            send_one(group * run + lax.rem(band, run))
        return carry

    def pipeline(sub, carry):
        @pl.when(sub < subs)
        def _():
            send_part(sub, 0)

        @pl.when(sub == lag)
        def _():
            pl.semaphore_wait(ready, width - 1)

        @pl.when(sub >= lag)
        def _():
            send_total(sub - lag, 0)
        return carry

    lax.fori_loop(0, subs + lag, pipeline, 0)

    own = pltpu.make_async_copy(total.at[pl.ds(2 * band, 2), :], landed.at[pl.ds(2 * band, 2), :], a_recv)
    own.start()
    pltpu.make_async_copy(landed, landed, a_recv).wait()

    lanes = lax.broadcasted_iota(jnp.int32, (bands // 4, 128), 1)
    for i in range(2):
        for f in range(2):
            for reim in range(2):
                value = jnp.zeros((bands // 4, 128), jnp.float32)
                for q in range(4):
                    x = landed[pl.ds(2 * q + i, bands // 4, stride=8), :]
                    for tr in range(2):
                        source = reim * 4 + tr * 2 + f
                        target = 2 * q + tr
                        moved = x if source == target else pltpu.roll(x, ((target - source) % 8) * 16, 1)
                        value = jnp.where(lanes // 16 == target, moved, value)
                for j in range(bands // 4):
                    out_ref[i, pl.ds(2 * f + reim, 1), pl.ds(j * 128, 128)] = value[j:j + 1, :]

    upward.wait_send()
    downward.wait_send()
    for sub in range(subs):
        for step in range(1, lons):
            over_lon(step, group_of(sub), sub).wait_send()
    others = pl.ds(0, per_lon - 2)
    pltpu.make_async_copy(total.at[others], total.at[others], a_send).wait()


def spectra(targets, qu, off, rb, cb, orders, bands, lons, subs=4, lag=3, unroll=256):
    V = pl.BlockSpec(memory_space=pltpu.VMEM)
    f32, bf16 = jnp.float32, jnp.bfloat16
    blocks = rb.shape[0]
    return pl.pallas_call(
        functools.partial(spectra_kernel, bands, lons, subs, lag, unroll),
        out_shape=jax.ShapeDtypeStruct((2, 4, bands * ROWS_DEV), f32),
        in_specs=[pl.BlockSpec(memory_space=pl.ANY)] * 6,
        out_specs=V,
        scratch_shapes=[
            pltpu.VMEM(targets.shape, jnp.int32),
            pltpu.VMEM(qu.shape, f32),
            pltpu.VMEM(off.shape, f32),
            pltpu.VMEM(rb.shape, jnp.int32),
            pltpu.VMEM(cb.shape, jnp.int32),
            pltpu.VMEM(orders.shape, jnp.int32),
            pltpu.VMEM((8, 128), jnp.int32),
            pltpu.SMEM((8, 128), jnp.int32),
            pltpu.VMEM((blocks + 1, 2 * TR, TC), f32),
            pltpu.VMEM((64, 2 * TR, TC), f32),
            pltpu.VMEM((2, 16, 2 * TR, TC), f32),
            pltpu.VMEM((1024, 128), f32),
            pltpu.VMEM((subs, 2, 512, 256), bf16),
            pltpu.VMEM((subs, 2, 256, 128), f32),
            pltpu.VMEM((subs, 2, 256, 128), f32),
            pltpu.VMEM((2, 256, 512), bf16),
            pltpu.VMEM((subs, lons, 256 // subs, 128), f32),
            pltpu.VMEM((subs, lons, 256 // subs, 128), f32),
            pltpu.VMEM((256, 128), f32),
            pltpu.VMEM((256, 128), f32),
            pltpu.SemaphoreType.REGULAR,
            pltpu.SemaphoreType.DMA((6,)),
            pltpu.SemaphoreType.DMA,
            pltpu.SemaphoreType.DMA((2,)),
            pltpu.SemaphoreType.DMA((2,)),
            pltpu.SemaphoreType.DMA((lons, subs)),
            pltpu.SemaphoreType.DMA((lons, subs)),
            pltpu.SemaphoreType.DMA,
            pltpu.SemaphoreType.DMA,
        ],
        compiler_params=pltpu.CompilerParams(collective_id=0, has_side_effects=True, vmem_limit_bytes=63 * 1024 * 1024),
    )(targets, qu, off, rb, cb, orders)


def body(qu_values, tap_offsets, row_base, col_base, tile_of_block, m_orders):
    bands = lax.axis_size("band")
    lons = lax.axis_size("lon")
    return spectra(tile_of_block.reshape(1, -1), qu_values, tap_offsets, row_base, col_base, m_orders.reshape(8, 128),
                   bands, lons)


def solution(mesh):
    placed = (
        P(None, ("band", "lon"), None),
        P(None, ("band", "lon"), None),
        P(("band", "lon"), None),
        P(("band", "lon"), None),
        P(("band", "lon")),
        P(),
    )
    return jax.shard_map(
        body, mesh=mesh, in_specs=placed, out_specs=P(("band", "lon"), None, None), check_vma=False
    )
```
